128 devices in a mesh: grp: 16 (over x, z), pr: 4 (over y), pc: 2 (over core).
Axes of the slice: x: 4, y: 4, z: 4, core: 2. Of those that a mesh axis runs over, the one named last changes fastest.
Arguments:
- pair_map: bfloat16 [1280, 1280, 128], P(('pr', 'pc'), 'grp'), may hold values from -6 to 6
- pair_mask: int32 [1280, 1280], P(('pr', 'pc'), 'grp'), may hold values 0 or 1
- input_gain: float32 [128], replicated, may hold values from 0.5 to 1.5
- input_bias: float32 [128], replicated, may hold values from -3 to 3
- input_weights: bfloat16 [128, 640], replicated, may hold values from -0.5 to 0.5
- output_gain: float32 [128], replicated, may hold values from 0.5 to 1.5
- output_bias: float32 [128], replicated, may hold values from -3 to 3
- output_weight: bfloat16 [128, 128], replicated, may hold values from -0.5 to 0.5
Outputs:
- update: bfloat16 [1280, 1280, 128], P(('pr', 'pc'), 'grp')
The draws below stay inside these ranges and needn't reach their ends.
All inputs are finite; a program needn't handle non-finite values. No bound on the sum of `pair_mask` on one device may be relied on, other than what follows from the above.
Results may differ from the reference program's by a relative error of at most 0.0059.
Values may be sent and summed in bfloat16 or wider, within the bound.
A program may use at most 128 MiB of HBM per device.

```python
import jax
import jax.numpy as jnp
from jax import lax

C = 128
N = 1280


def place_ends(drawn, key, least, largest):
    index_at = [jax.random.randint(jax.random.fold_in(key, axis), (), 0, length) for axis, length in enumerate(drawn.shape)]
    longest = drawn.shape.index(max(drawn.shape))
    beside = index_at[:longest] + [(index_at[longest] + 1) % drawn.shape[longest]] + index_at[longest + 1:]
    return drawn.at[tuple(index_at)].set(least).at[tuple(beside)].set(largest)


def levels(key, dims, shards, smallest, largest):
    loudness = 1.0
    for position, blocks in shards:
        steps = jax.random.uniform(jax.random.fold_in(jax.random.fold_in(key, 6), position), (blocks,), jnp.float32, smallest / len(shards), largest / len(shards))
        loudness = loudness * jnp.repeat(jnp.exp(steps), dims[position] // blocks).reshape((-1,) + (1,) * (len(dims) - 1 - position))
    return loudness


def scatter_about(key, shape, width, most, pieces=(), kind=jnp.bfloat16):
    array = width * jax.random.normal(key, shape, jnp.float32)
    if pieces:
        array = array * levels(key, shape, pieces, -0.22, 0.18)
    return jnp.clip(array, -most, most).astype(kind)


def setup_inputs(seed: int = 0) -> dict:
    key_of = jax.random.split(jax.random.key(seed), 9)
    return {
        "pair_map": scatter_about(key_of[0], (N, N, C), 1.0, 6.0, ((0, 8), (1, 16))),
        "pair_mask": place_ends((jax.random.randint(key_of[1], (N, N), 0, 8) < 7).astype(jnp.int32), jax.random.fold_in(key_of[1], 1), 0, 1),
        "input_gain": jnp.clip(1.0 + 0.1 * jax.random.normal(key_of[2], (C,), jnp.float32), 0.5, 1.5),
        "input_bias": scatter_about(key_of[3], (C,), 0.5, 3.0, (), jnp.float32),
        "input_weights": scatter_about(key_of[4], (C, 5 * C), C ** -0.5, 0.5),
        "output_gain": jnp.clip(1.0 + 0.1 * jax.random.normal(key_of[5], (C,), jnp.float32), 0.5, 1.5),
        "output_bias": scatter_about(key_of[6], (C,), 0.5, 3.0, (), jnp.float32),
        "output_weight": scatter_about(key_of[7], (C, C), C ** -0.5, 0.5),
    }


epsilon = 1e-05

def layer_norm(values, scaling, offset, along):
    center = lax.optimization_barrier(jnp.mean(values, axis=along, keepdims=True))
    shifted = values - center
    spread = lax.optimization_barrier(jnp.mean(shifted * shifted, axis=along, keepdims=True))
    return shifted * lax.rsqrt(spread + epsilon) * scaling + offset

def reference(pair_map, pair_mask, input_gain, input_bias, input_weights, output_gain, output_bias, output_weight):
    row_count = 128
    block_total = N // row_count
    starts = jnp.arange(block_total, dtype=jnp.int32) * row_count
    weights_wide = input_weights.astype(jnp.float32)
    highest = lax.Precision.HIGHEST

    def normalize_rows(start):
        rows = lax.dynamic_slice_in_dim(pair_map, start, row_count, 0).astype(jnp.float32)
        rounded = layer_norm(rows, input_gain, input_bias, -1).astype(jnp.bfloat16)
        rounded = lax.optimization_barrier(rounded)
        return rounded.astype(jnp.float32).reshape(-1, C)

    def project(start):
        normed = normalize_rows(start)
        masking = lax.dynamic_slice_in_dim(pair_mask, start, row_count, 0).astype(jnp.float32).reshape(-1, 1)
        results = []
        for column_start in (0, 2):
            value_part = jnp.dot(normed, weights_wide[:, column_start * C:(column_start + 1) * C], precision=highest)
            gate_part = jnp.dot(normed, weights_wide[:, (column_start + 1) * C:(column_start + 2) * C], precision=highest)
            side = (masking * jax.nn.sigmoid(gate_part) * value_part).astype(jnp.bfloat16)
            results.append(side.reshape(row_count, N, C).transpose(2, 0, 1))
        return (results[0], results[1])
    left_blocks, right_blocks = lax.map(project, starts)
    left_all = jnp.transpose(left_blocks, (1, 0, 2, 3)).reshape(C, N, N)
    right_all = jnp.transpose(right_blocks, (1, 0, 2, 3)).reshape(C, N, N)

    def channel_product(pair):
        left_one, right_one = pair
        return jnp.dot(left_one.astype(jnp.float32), right_one.astype(jnp.float32).T, precision=highest).astype(jnp.bfloat16)
    triangle = lax.map(channel_product, (left_all, right_all))

    def finish(start):
        normed = normalize_rows(start)
        gate_out = jax.nn.sigmoid(jnp.dot(normed, weights_wide[:, 4 * C:], precision=highest)).reshape(row_count, N, C)
        portion = lax.dynamic_slice_in_dim(triangle, start, row_count, 1).astype(jnp.float32)
        settled = layer_norm(portion, output_gain[:, None, None], output_bias[:, None, None], 0).astype(jnp.bfloat16)
        settled = lax.optimization_barrier(settled)
        mixed = jnp.einsum('cij,cd->ijd', settled.astype(jnp.float32), output_weight.astype(jnp.float32), precision=highest)
        return (gate_out * mixed).astype(jnp.bfloat16)
    update = lax.map(finish, starts).reshape(N, N, C)
    return update
```

```python
import jax
import jax.numpy as jnp
from jax import lax
from jax.experimental import pallas as pl
from jax.experimental.pallas import tpu as pltpu
from jax.sharding import PartitionSpec as P

MESH = pl.DeviceIdType.MESH
F32 = jnp.float32
BF16 = jnp.bfloat16
epsilon = 1e-05

I = 160
K = 80
C = 128
G = 16
A = 8
ROWS = 104
N = 1280


def mod(value, by):
    return lax.rem(value, by)


def kernel(
    x_ref,
    mask_ref,
    gain_ref,
    bias_ref,
    proj_ref,
    gatew_ref,
    ogain_ref,
    obias_ref,
    ow_ref,
    o_ref,
    normed,
    gates,
    swap,
    out_l,
    out_r,
    in_l,
    in_r,
    rest_l,
    rest_r,
    right_t,
    out_t,
    in_t,
    send_sem,
    recv_sem,
):
    g = lax.axis_index("grp")
    y = lax.axis_index("pr")
    core = lax.axis_index("pc")
    x, z = g // 4, mod(g, 4)
    a = y * 2 + core
    quarter = mod(a, 4)
    mine = g * A + a

    def partner(step):
        v = mod(step * 11, 128)
        px = mod(x + mod(v, 4), 4)
        py = mod(y + mod(v // 4, 4), 4)
        pcore = mod(core + mod(v // 16, 2), 2)
        pz = mod(z + v // 32, 4)
        return px * 4 + pz, py, pcore

    barrier = pltpu.get_barrier_semaphore()

    def greet(step, carry):
        pg, py, pcore = partner(step)
        pl.semaphore_signal(
            barrier, inc=1, device_id={"grp": pg, "pr": py, "pc": pcore}, device_id_type=MESH
        )
        return carry

    lax.fori_loop(1, 128, greet, 0)

    lane_group = lax.broadcasted_iota(jnp.int32, (8, 128), 1) // 32

    def by_group(parts):
        group = lax.broadcasted_iota(jnp.int32, parts[0].shape, 1) // 32
        return jnp.where(
            group == 0, parts[0], jnp.where(group == 1, parts[1], jnp.where(group == 2, parts[2], parts[3]))
        )

    def token(s, r, low):
        n = mod(quarter - s + 4, 4)
        return n * 16 + r if low else 64 + n * 4 + r

    def normalize(k, carry):
        rows = x_ref[k].astype(F32)
        center = jnp.mean(rows, axis=-1, keepdims=True)
        shifted = rows - center
        spread = jnp.mean(shifted * shifted, axis=-1, keepdims=True)
        normed[k] = (
            shifted * lax.rsqrt(spread + epsilon) * gain_ref[...] + bias_ref[...]
        ).astype(BF16)
        return carry

    lax.fori_loop(0, K, normalize, 0)

    def gated(tokens, weights, mask_rows):
        both = lax.dot_general(
            weights, tokens, (((1,), (1,)), ((), ())), preferred_element_type=F32
        )
        value, gate = both[:C], both[C:]
        return value * jax.nn.sigmoid(gate) * mask_rows

    def unswap(store, rows, at):
        def one(c, carry):
            store[c, pl.ds(at, rows), :] = swap[pl.ds(c, rows, stride=C), :].astype(BF16)
            return carry

        lax.fori_loop(0, C, one, 0, unroll=8)

    def rest_tokens(r, low):
        return jnp.concatenate(
            [normed[token(s, r, low), 128:, :] for s in range(4)], axis=0
        )

    def rest_mask(r, low):
        return by_group([mask_ref[1, pl.ds(token(s, r, low), 1), :] for s in range(4)])

    def project(first, store):
        weights = proj_ref[first : first + 2 * C, :]

        def block(b, carry):
            def pair(p, carry):
                k = b * 16 + p * 2
                tokens = normed[pl.ds(k, 2), 0:128, :].reshape(256, C)
                rows = mask_ref[0, pl.ds(k, 2), :]
                result = gated(
                    tokens, weights, jnp.concatenate([rows[0:1], rows[1:2]], axis=1)
                )
                swap[pl.ds(p * 256, C), :] = result[:, :128]
                swap[pl.ds(p * 256 + C, C), :] = result[:, 128:]
                return carry

            lax.fori_loop(0, 8, pair, 0)
            unswap(store, 16, pl.multiple_of(b * 16, 16))
            return carry

        lax.fori_loop(0, 5, block, 0)

        for low, pairs, rows, at in ((True, 8, 16, 80), (False, 2, 8, 96)):

            def rest(p, carry):
                r = p * 2
                tokens = jnp.concatenate([rest_tokens(r, low), rest_tokens(r + 1, low)], axis=0)
                result = gated(
                    tokens,
                    weights,
                    jnp.concatenate([rest_mask(r, low), rest_mask(r + 1, low)], axis=1),
                )
                swap[pl.ds(p * 256, C), :] = result[:, :128]
                swap[pl.ds(p * 256 + C, C), :] = result[:, 128:]
                return carry

            lax.fori_loop(0, pairs, rest, 0)
            unswap(store, rows, at)

    def send_side(source, target, which):
        def one(step, carry):
            pg, py, pcore = partner(step)
            pltpu.make_async_remote_copy(
                src_ref=source.at[pg * A + py * 2 + pcore],
                dst_ref=target.at[a, g],
                send_sem=send_sem.at[which],
                recv_sem=recv_sem.at[which],
                device_id={"grp": pg, "pr": py, "pc": pcore},
                device_id_type=MESH,
            ).start()
            return carry

        pltpu.make_async_copy(source.at[mine], target.at[a, g], recv_sem.at[which]).start()
        lax.fori_loop(1, 128, one, 0)

    def wait_all(buffer, semaphore):
        pltpu.make_async_copy(buffer, buffer, semaphore).wait()

    project(2 * C, out_r)
    pl.semaphore_wait(barrier, 127)
    send_side(out_r, in_r, 0)
    project(0, out_l)
    send_side(out_l, in_l, 1)

    def open_gate(p, carry):
        tokens = normed[pl.ds(p * 2, 2)].reshape(2 * I, C)
        gates[pl.ds(p * 2, 2)] = jax.nn.sigmoid(
            jnp.dot(tokens, gatew_ref[...], preferred_element_type=F32)
        ).reshape(2, I, C)
        return carry

    lax.fori_loop(0, K // 2, open_gate, 0)

    def spread_rest(arrived, rest):
        def one(step, carry):
            h, sg = step // G, mod(step, G)
            parts = [arrived[4 * h + t, sg, 80:96, :].astype(F32) for t in range(4)]
            tails = [arrived[4 * h + t, sg, 96:104, :].astype(F32) for t in range(4)]
            at = sg * K
            ends = []
            for n in range(4):
                rows = by_group([parts[(s + n) % 4] for s in range(4)])
                tail = by_group([tails[(s + n) % 4] for s in range(4)])
                if n:
                    rows = pltpu.roll(rows, 32 * n, 1)
                    tail = pltpu.roll(tail, 32 * n, 1)
                rest[h, pl.ds(pl.multiple_of(at + n * 16, 16), 16), :] = rows.astype(BF16)
                ends.append(tail)
            upper = lax.broadcasted_iota(jnp.int32, (8, 128), 0) < 4
            joined = jnp.concatenate(
                [
                    jnp.where(upper, ends[0], pltpu.roll(ends[1], 4, 0)),
                    jnp.where(upper, ends[2], pltpu.roll(ends[3], 4, 0)),
                ],
                axis=0,
            )
            rest[h, pl.ds(pl.multiple_of(at + 64, 16), 16), :] = joined.astype(BF16)
            return carry

        lax.fori_loop(0, 2 * G, one, 0)

    wait_all(in_r, recv_sem.at[0])
    spread_rest(in_r, rest_r)

    def turn_main(b, carry):
        tile = in_r[b, :, 0:K, :].reshape(N, 128)
        right_t[pl.ds(pl.multiple_of(b * I, 32), 128), :] = tile.T
        return carry

    lax.fori_loop(0, A, turn_main, 0)

    def turn_rest(h, carry):
        turned = rest_r[h].T
        for t in range(4):
            right_t[pl.ds(pl.multiple_of((4 * h + t) * I + 128, 32), 32), :] = turned[
                32 * t : 32 * t + 32
            ]
        return carry

    lax.fori_loop(0, 2, turn_rest, 0)

    wait_all(in_l, recv_sem.at[1])
    spread_rest(in_l, rest_l)

    def rest_product(m, carry):
        rows = right_t[pl.ds(pl.multiple_of(m * 320, 32), 320), :]
        columns = jnp.concatenate([rest_l[0], rest_l[1]], axis=1)
        product = jnp.dot(rows, columns, preferred_element_type=F32)
        for h in range(2):
            for sg in range(4):
                block = product[sg * K : (sg + 1) * K, h * 128 : (h + 1) * 128]
                mains, tails = [], []
                for n in range(4):
                    main = block[n * 16 : (n + 1) * 16]
                    tail = block[64 + 8 * (n // 2) : 72 + 8 * (n // 2)]
                    if n % 2:
                        tail = pltpu.roll(tail, 4, 0)
                    if n:
                        main = pltpu.roll(main, 128 - 32 * n, 1)
                        tail = pltpu.roll(tail, 128 - 32 * n, 1)
                    mains.append(main)
                    tails.append(tail)
                for t in range(4):
                    out_t[m * 4 + sg, 4 * h + t, 80:96, :] = by_group(
                        [mains[(t - s) % 4] for s in range(4)]
                    ).astype(BF16)
                    out_t[m * 4 + sg, 4 * h + t, 96:104, :] = by_group(
                        [tails[(t - s) % 4] for s in range(4)]
                    ).astype(BF16)
        return carry

    lax.fori_loop(0, 4, rest_product, 0)

    def main_product(step, carry):
        ty = mod(y + step, 4)

        def part(m, carry):
            rows = right_t[pl.ds(pl.multiple_of(m * 320, 32), 320), :]
            columns = jnp.concatenate(
                [in_l[2 * ty + i, :, 0:K, :].reshape(N, 128) for i in range(2)], axis=1
            )
            product = jnp.dot(rows, columns, preferred_element_type=F32).astype(BF16)
            for i in range(2):
                out_t[pl.ds(m * 4, 4), 2 * ty + i, 0:K, :] = product[
                    :, i * 128 : (i + 1) * 128
                ].reshape(4, K, 128)
            return carry

        lax.fori_loop(0, 4, part, 0)
        return carry

    lax.fori_loop(0, 4, main_product, 0)

    def send_back(step, carry):
        pg, py, pcore = partner(step)
        pltpu.make_async_remote_copy(
            src_ref=out_t.at[pg, py * 2 + pcore],
            dst_ref=in_t.at[mine],
            send_sem=send_sem.at[2],
            recv_sem=recv_sem.at[2],
            device_id={"grp": pg, "pr": py, "pc": pcore},
            device_id_type=MESH,
        ).start()
        return carry

    pltpu.make_async_copy(out_t.at[g, a], in_t.at[mine], recv_sem.at[2]).start()
    lax.fori_loop(1, 128, send_back, 0)

    wait_all(in_t, recv_sem.at[2])

    def settle(r, rows):
        values = swap[pl.ds(r, C, stride=rows), :]
        center = jnp.mean(values, axis=0, keepdims=True)
        shifted = values - center
        spread = jnp.mean(shifted * shifted, axis=0, keepdims=True)
        settled = (
            shifted * lax.rsqrt(spread + epsilon) * ogain_ref[...] + obias_ref[...]
        ).astype(BF16)
        return lax.dot_general(
            settled, ow_ref[...], (((0,), (0,)), ((), ())), preferred_element_type=F32
        )

    def widen(at, rows):
        def one(c, carry):
            swap[pl.ds(pl.multiple_of(c * rows, 8), rows), :] = in_t[c, pl.ds(at, rows), :].astype(F32)
            return carry

        lax.fori_loop(0, C, one, 0, unroll=8)

    def finish(b, carry):
        widen(pl.multiple_of(b * 16, 16), 16)

        def one(r, carry):
            j = b * 16 + r
            o_ref[j, 0:128, :] = (gates[j, 0:128, :] * settle(r, 16)).astype(BF16)
            return carry

        lax.fori_loop(0, 16, one, 0)
        return carry

    lax.fori_loop(0, 5, finish, 0)

    for low, count, rows, at in ((True, 16, 16, 80), (False, 4, 8, 96)):
        widen(at, rows)

        def one_rest(r, carry):
            mixed = settle(r, rows)
            for s in range(4):
                j = token(s, r, low)
                o_ref[j, 128:, :] = (
                    gates[j, 128:, :] * mixed[32 * s : 32 * s + 32]
                ).astype(BF16)
            return carry

        lax.fori_loop(0, count, one_rest, 0)

    for which, buffer in ((0, out_r), (1, out_l), (2, in_t)):
        sent = buffer.at[pl.ds(0, 127)]
        pltpu.make_async_copy(sent, sent, send_sem.at[which]).wait()


def per_device(
    pair_map,
    pair_mask,
    input_gain,
    input_bias,
    input_weights,
    output_gain,
    output_bias,
    output_weight,
):
    turned = jnp.transpose(pair_map, (1, 0, 2))
    mask = pair_mask.astype(F32).T
    masks = jnp.stack([mask[:, :128], jnp.tile(mask[:, 128:], (1, 4))])
    weights = input_weights[:, : 4 * C].T
    gate_weights = input_weights[:, 4 * C :]
    gains = jnp.broadcast_to(output_gain[:, None], (C, 128))
    offsets = jnp.broadcast_to(output_bias[:, None], (C, 128))
    vmem = pl.BlockSpec(memory_space=pltpu.VMEM)
    result = pl.pallas_call(
        kernel,
        out_shape=jax.ShapeDtypeStruct((K, I, C), BF16),
        in_specs=[vmem] * 9,
        out_specs=vmem,
        scratch_shapes=[
            pltpu.VMEM((K, I, C), BF16),
            pltpu.VMEM((K, I, C), F32),
            pltpu.VMEM((16 * C, 128), F32),
            pltpu.VMEM((C, ROWS, 128), BF16),
            pltpu.VMEM((C, ROWS, 128), BF16),
            pltpu.VMEM((A, G, ROWS, 128), BF16),
            pltpu.VMEM((A, G, ROWS, 128), BF16),
            pltpu.VMEM((2, N, 128), BF16),
            pltpu.VMEM((2, N, 128), BF16),
            pltpu.VMEM((N, N), BF16),
            pltpu.VMEM((G, A, ROWS, 128), BF16),
            pltpu.VMEM((C, ROWS, 128), BF16),
            pltpu.SemaphoreType.DMA((3,)),
            pltpu.SemaphoreType.DMA((3,)),
        ],
        compiler_params=pltpu.CompilerParams(
            collective_id=0, has_side_effects=True, vmem_limit_bytes=56 * 2**20
        ),
        cost_estimate=pl.CostEstimate(
            flops=6_500_000_000, bytes_accessed=16_000_000, transcendentals=5_000_000
        ),
    )(
        turned,
        masks,
        input_gain[None],
        input_bias[None],
        weights,
        gate_weights,
        gains,
        offsets,
        output_weight,
    )
    return jnp.transpose(result, (1, 0, 2))


def solution(mesh):
    return jax.shard_map(
        per_device,
        mesh=mesh,
        in_specs=(
            P(("pr", "pc"), "grp", None),
            P(("pr", "pc"), "grp"),
            P(),
            P(),
            P(),
            P(),
            P(),
            P(),
        ),
        out_specs=P(("pr", "pc"), "grp", None),
        check_vma=False,
    )
```

```python
import jax
import jax.numpy as jnp
from jax import lax
from jax.experimental import pallas as pl
from jax.experimental.pallas import tpu as pltpu
from jax.sharding import PartitionSpec as P

MESH = pl.DeviceIdType.MESH
F32 = jnp.float32
BF16 = jnp.bfloat16
epsilon = 1e-05

I = 160
K = 80
C = 128
G = 16
A = 8
N = 1280
REST = 24
FIRST = 48
R_MAIN, R_REST, L_REST, L_MAIN, T_REST, T_FIRST, T_LAST = range(7)


def kernel(
    x_ref,
    mask_ref,
    gain_ref,
    bias_ref,
    weights_ref,
    ogain_ref,
    obias_ref,
    ow_ref,
    o_ref,
    wide,
    normed,
    gates,
    swap,
    proj,
    mask_main,
    mask_rest,
    scaling,
    out_l,
    out_r,
    out_t,
    out_l_rest,
    out_r_rest,
    out_t_rest,
    in_l,
    in_r,
    in_t,
    in_l_rest,
    in_r_rest,
    in_t_rest,
    rest_l,
    rest_r,
    right_t,
    send_sem,
    recv_sem,
):
    g = lax.axis_index("grp")
    y = lax.axis_index("pr")
    core = lax.axis_index("pc")
    x, z = g // 4, g % 4
    a = y * 2 + core
    quarter = a % 4
    mine = g * A + a

    def partner(step):
        v = (step * 47) % 128
        px = (x + (0 + v % 4 + (v % 4) // 2 - 2 * ((v % 4) // 3))) % 4
        pcore = (core + (v // 4) % 2) % 2
        py = (y + (v // 8) % 4) % 4
        pz = (z + v // 32) % 4
        return px * 4 + pz, py, pcore

    def place(pg, py, pcore):
        return {"grp": pg, "pr": py, "pc": pcore}

    barrier = pltpu.get_barrier_semaphore()

    def greet(step, carry):
        pl.semaphore_signal(
            barrier, inc=1, device_id=place(*partner(step)), device_id_type=MESH
        )
        return carry

    lax.fori_loop(1, 128, greet, 0)

    def by_group(parts):
        group = lax.broadcasted_iota(jnp.int32, parts[0].shape, 1) // 32
        return jnp.where(
            group == 0,
            parts[0],
            jnp.where(group == 1, parts[1], jnp.where(group == 2, parts[2], parts[3])),
        )

    def token(s, r, low):
        n = (quarter - s + 4) % 4
        return n * 16 + r if low else 64 + n * 4 + r

    def by_16(value):
        return pl.multiple_of(value, 16)

    for part in range(4):
        columns = weights_ref[:, part * C : (part + 1) * C].astype(F32)
        proj[part * C : (part + 1) * C, :] = columns.T.astype(BF16)
    scaling[0] = jnp.broadcast_to(ogain_ref[...], (C, 128)).T
    scaling[1] = jnp.broadcast_to(obias_ref[...], (C, 128)).T
    mask = mask_ref[...].astype(F32).T
    mask_main[...] = mask[:, :128]
    mask_rest[...] = jnp.concatenate([mask[:, 128:]] * 4, axis=1)
    ones = jnp.full((256, 128), 1 / 128, BF16)

    def normalize(b):
        def rows(i, carry):
            block = x_ref[pl.ds(i * 8, 8), pl.ds(by_16(b * 16), 16), :].reshape(128, C)
            center = jnp.dot(block, ones[:128], preferred_element_type=F32)
            shifted = block.astype(F32) - center
            squares = shifted * shifted
            high = squares.astype(BF16)
            low = (squares - high.astype(F32)).astype(BF16)
            spread = jnp.dot(
                jnp.concatenate([high, low], axis=1), ones, preferred_element_type=F32
            )
            wide[pl.ds(i * 128, 128), :] = (
                shifted * lax.rsqrt(spread + epsilon) * gain_ref[...] + bias_ref[...]
            )
            return carry

        lax.fori_loop(0, I // 8, rows, 0, unroll=2)

        def turn(k, carry):
            normed[b * 16 + k] = wide[pl.ds(k, I, stride=16), :].astype(BF16)
            return carry

        lax.fori_loop(0, 16, turn, 0, unroll=2)

    def gated(tokens, weights, mask_rows):
        both = lax.dot_general(
            weights, tokens, (((1,), (1,)), ((), ())), preferred_element_type=F32
        )
        value, gate = both[:C], both[C:]
        return value * jax.nn.sigmoid(gate) * mask_rows

    def unswap(store, rows, at):
        def one(c, carry):
            store[c, pl.ds(at, rows), :] = swap[pl.ds(c, rows, stride=C), :].astype(BF16)
            return carry

        lax.fori_loop(0, C, one, 0, unroll=8)

    def project_main(b, first, store):
        weights = proj[first : first + 2 * C, :]

        def pair(p, carry):
            k = b * 16 + p * 2
            tokens = normed[pl.ds(k, 2), 0:128, :].reshape(256, C)
            rows = mask_main[pl.ds(k, 2), :]
            result = gated(tokens, weights, jnp.concatenate([rows[0:1], rows[1:2]], axis=1))
            swap[pl.ds(p * 256, C), :] = result[:, :128]
            swap[pl.ds(p * 256 + C, C), :] = result[:, 128:]
            return carry

        lax.fori_loop(0, 8, pair, 0)
        unswap(store, 16, by_16(b * 16))

    def rest_tokens(r, low):
        return jnp.concatenate([normed[token(s, r, low), 128:, :] for s in range(4)], axis=0)

    def rest_mask(r, low):
        return by_group([mask_rest[pl.ds(token(s, r, low), 1), :] for s in range(4)])

    def project_rest(first, store):
        weights = proj[first : first + 2 * C, :]
        for low, pairs, rows, at in ((True, 8, 16, 0), (False, 2, 8, 16)):

            def rest(p, carry):
                r = p * 2
                tokens = jnp.concatenate([rest_tokens(r, low), rest_tokens(r + 1, low)], axis=0)
                result = gated(
                    tokens,
                    weights,
                    jnp.concatenate([rest_mask(r, low), rest_mask(r + 1, low)], axis=1),
                )
                swap[pl.ds(p * 256, C), :] = result[:, :128]
                swap[pl.ds(p * 256 + C, C), :] = result[:, 128:]
                return carry

            lax.fori_loop(0, pairs, rest, 0)
            unswap(store, rows, at)

    def send_round(source, target, which):
        def one(step, carry):
            pg, py, pcore = partner(step)
            pltpu.make_async_remote_copy(
                src_ref=source(pg, py * 2 + pcore),
                dst_ref=target,
                send_sem=send_sem.at[which],
                recv_sem=recv_sem.at[which],
                device_id=place(pg, py, pcore),
                device_id_type=MESH,
            ).start()
            return carry

        pltpu.make_async_copy(source(g, a), target, recv_sem.at[which]).start()
        lax.fori_loop(1, 128, one, 0)

    def wait_all(buffer, semaphore):
        pltpu.make_async_copy(buffer, buffer, semaphore).wait()

    def send_main(b, store, target, which):
        send_round(
            lambda pg, pa: store.at[pg * A + pa, pl.ds(by_16(b * 16), 16)],
            target.at[a, pl.ds(by_16(g * K + b * 16), 16)],
            which,
        )

    def right_block(b, carry):
        normalize(b)
        project_main(b, 2 * C, out_r)

        @pl.when(b == 0)
        def _():
            pl.semaphore_wait(barrier, 127)

        send_main(b, out_r, in_r, R_MAIN)
        return carry

    lax.fori_loop(0, 5, right_block, 0)
    project_rest(2 * C, out_r_rest)
    send_round(lambda pg, pa: out_r_rest.at[pg * A + pa], in_r_rest.at[a, g], R_REST)
    project_rest(0, out_l_rest)
    send_round(lambda pg, pa: out_l_rest.at[pg * A + pa], in_l_rest.at[a, g], L_REST)

    def left_block(b, carry):
        project_main(b, 0, out_l)
        send_main(b, out_l, in_l, L_MAIN)
        return carry

    lax.fori_loop(0, 5, left_block, 0)

    def open_gate(p, carry):
        tokens = normed[pl.ds(p * 2, 2)].reshape(2 * I, C)
        gates[pl.ds(p * 2, 2)] = jax.nn.sigmoid(
            jnp.dot(tokens, weights_ref[:, 4 * C :], preferred_element_type=F32)
        ).reshape(2, I, C)
        return carry

    lax.fori_loop(0, K // 2, open_gate, 0)

    def spread_rest(arrived, rest):
        def one(step, carry):
            h, sg = step // G, step % G
            parts = [arrived[4 * h + t, sg, 0:16, :].astype(F32) for t in range(4)]
            tails = [arrived[4 * h + t, sg, 16:24, :].astype(F32) for t in range(4)]
            at = sg * K
            ends = []
            for n in range(4):
                rows = by_group([parts[(s + n) % 4] for s in range(4)])
                tail = by_group([tails[(s + n) % 4] for s in range(4)])
                if n:
                    rows = pltpu.roll(rows, 32 * n, 1)
                    tail = pltpu.roll(tail, 32 * n, 1)
                rest[h, pl.ds(by_16(at + n * 16), 16), :] = rows.astype(BF16)
                ends.append(tail)
            upper = lax.broadcasted_iota(jnp.int32, (8, 128), 0) < 4
            joined = jnp.concatenate(
                [
                    jnp.where(upper, ends[0], pltpu.roll(ends[1], 4, 0)),
                    jnp.where(upper, ends[2], pltpu.roll(ends[3], 4, 0)),
                ],
                axis=0,
            )
            rest[h, pl.ds(by_16(at + 64), 16), :] = joined.astype(BF16)
            return carry

        lax.fori_loop(0, 2 * G, one, 0)

    wait_all(in_r, recv_sem.at[R_MAIN])

    def turn_main(b, carry):
        right_t[pl.ds(pl.multiple_of(b * I, 32), 128), :] = in_r[b].T
        return carry

    lax.fori_loop(0, A, turn_main, 0)

    wait_all(in_r_rest, recv_sem.at[R_REST])
    spread_rest(in_r_rest, rest_r)

    def turn_rest(h, carry):
        turned = rest_r[h].T
        for t in range(4):
            right_t[pl.ds(pl.multiple_of((4 * h + t) * I + 128, 32), 32), :] = turned[
                32 * t : 32 * t + 32
            ]
        return carry

    lax.fori_loop(0, 2, turn_rest, 0)

    wait_all(in_l_rest, recv_sem.at[L_REST])
    spread_rest(in_l_rest, rest_l)

    def rest_product(m, carry):
        rows = right_t[pl.ds(pl.multiple_of(m * 320, 32), 320), :]
        columns = jnp.concatenate([rest_l[0], rest_l[1]], axis=1)
        product = jnp.dot(rows, columns, preferred_element_type=F32)
        for h in range(2):
            for sg in range(4):
                block = product[sg * K : (sg + 1) * K, h * 128 : (h + 1) * 128]
                mains, tails = [], []
                for n in range(4):
                    main = block[n * 16 : (n + 1) * 16]
                    tail = block[64 + 8 * (n // 2) : 72 + 8 * (n // 2)]
                    if n % 2:
                        tail = pltpu.roll(tail, 4, 0)
                    if n:
                        main = pltpu.roll(main, 128 - 32 * n, 1)
                        tail = pltpu.roll(tail, 128 - 32 * n, 1)
                    mains.append(main)
                    tails.append(tail)
                for t in range(4):
                    out_t_rest[m * 4 + sg, 4 * h + t, 0:16, :] = by_group(
                        [mains[(t - s) % 4] for s in range(4)]
                    ).astype(BF16)
                    out_t_rest[m * 4 + sg, 4 * h + t, 16:24, :] = by_group(
                        [tails[(t - s) % 4] for s in range(4)]
                    ).astype(BF16)
        return carry

    lax.fori_loop(0, 4, rest_product, 0)
    send_round(lambda pg, pa: out_t_rest.at[pg, pa], in_t_rest.at[mine], T_REST)

    wait_all(in_l, recv_sem.at[L_MAIN])

    def main_product(step, carry):
        i, j = step % 4, step // 4
        dx = (1 + 2 * i + i // 2) % 4
        dy = (3 * dx + j) % 4
        tx, ty = (x + dx) % 4, (y + dy) % 4
        rows = right_t[pl.ds(pl.multiple_of(tx * 320, 32), 320), :]
        columns = jnp.concatenate([in_l[2 * ty], in_l[2 * ty + 1]], axis=1)
        product = jnp.dot(rows, columns, preferred_element_type=F32).astype(BF16)
        for h in range(2):
            out_t[pl.ds(tx * 4, 4), 2 * ty + h] = product[
                :, h * 128 : (h + 1) * 128
            ].reshape(4, K, 128)

        def send(q, carry):
            pg, pcore = tx * 4 + (z + q // 2) % 4, (core + q % 2) % 2
            source = out_t.at[pg, 2 * ty + pcore, pl.ds(0, FIRST)]
            target = in_t.at[mine, pl.ds(0, FIRST)]
            own = (dx == 0) & (dy == 0) & (q == 0)

            @pl.when(own)
            def _():
                pltpu.make_async_copy(source, target, recv_sem.at[T_FIRST]).start()

            @pl.when(jnp.logical_not(own))
            def _():
                pltpu.make_async_remote_copy(
                    src_ref=source,
                    dst_ref=target,
                    send_sem=send_sem.at[T_FIRST],
                    recv_sem=recv_sem.at[T_FIRST],
                    device_id=place(pg, ty, pcore),
                    device_id_type=MESH,
                ).start()

            return carry

        lax.fori_loop(0, 8, send, 0)
        return carry

    lax.fori_loop(0, 16, main_product, 0)
    last = pl.ds(FIRST, K - FIRST)
    send_round(lambda pg, pa: out_t.at[pg, pa, last], in_t.at[mine, last], T_LAST)

    def settle(r, rows):
        values = swap[pl.ds(r, C, stride=rows), :]
        center = jnp.mean(values, axis=0, keepdims=True)
        shifted = values - center
        spread = jnp.mean(shifted * shifted, axis=0, keepdims=True)
        settled = (shifted * lax.rsqrt(spread + epsilon) * scaling[0] + scaling[1]).astype(BF16)
        return lax.dot_general(
            settled, ow_ref[...], (((0,), (0,)), ((), ())), preferred_element_type=F32
        )

    def widen(arrived, at, rows):
        def one(c, carry):
            swap[pl.ds(pl.multiple_of(c * rows, 8), rows), :] = arrived[
                c, pl.ds(at, rows), :
            ].astype(F32)
            return carry

        lax.fori_loop(0, C, one, 0, unroll=8)

    def finish(b, carry):
        widen(in_t, by_16(b * 16), 16)

        def one(r, carry):
            j = b * 16 + r
            o_ref[j, 0:128, :] = (gates[j, 0:128, :] * settle(r, 16)).astype(BF16)
            return carry

        lax.fori_loop(0, 16, one, 0, unroll=4)
        return carry

    wait_all(in_t_rest, recv_sem.at[T_REST])
    for low, count, rows, at in ((True, 16, 16, 0), (False, 4, 8, 16)):
        widen(in_t_rest, at, rows)

        def one_rest(r, carry):
            mixed = settle(r, rows)
            for s in range(4):
                j = token(s, r, low)
                o_ref[j, 128:, :] = (
                    gates[j, 128:, :] * mixed[32 * s : 32 * s + 32]
                ).astype(BF16)
            return carry

        lax.fori_loop(0, count, one_rest, 0, unroll=4)

    wait_all(in_t.at[:, pl.ds(0, FIRST)], recv_sem.at[T_FIRST])
    lax.fori_loop(0, FIRST // 16, finish, 0)
    wait_all(in_t.at[:, last], recv_sem.at[T_LAST])
    lax.fori_loop(FIRST // 16, K // 16, finish, 0)

    for which, buffer in (
        (R_MAIN, out_r),
        (R_REST, out_r_rest),
        (L_REST, out_l_rest),
        (L_MAIN, out_l),
        (T_REST, in_t_rest),
        (T_FIRST, in_t.at[:, pl.ds(0, FIRST)]),
        (T_LAST, in_t.at[:, last]),
    ):
        wait_all(buffer.at[pl.ds(0, 127)], send_sem.at[which])


def per_device(
    pair_map,
    pair_mask,
    input_gain,
    input_bias,
    input_weights,
    output_gain,
    output_bias,
    output_weight,
):
    vmem = pl.BlockSpec(memory_space=pltpu.VMEM)
    result = pl.pallas_call(
        kernel,
        out_shape=jax.ShapeDtypeStruct((K, I, C), BF16),
        in_specs=[vmem] * 8,
        out_specs=vmem,
        scratch_shapes=[
            pltpu.VMEM((I * 16, C), F32),
            pltpu.VMEM((K, I, C), BF16),
            pltpu.VMEM((K, I, C), F32),
            pltpu.VMEM((16 * C, 128), F32),
            pltpu.VMEM((4 * C, C), BF16),
            pltpu.VMEM((K, 128), F32),
            pltpu.VMEM((K, 128), F32),
            pltpu.VMEM((2, C, 128), F32),
            pltpu.VMEM((C, K, 128), BF16),
            pltpu.VMEM((C, K, 128), BF16),
            pltpu.VMEM((G, A, K, 128), BF16),
            pltpu.VMEM((C, REST, 128), BF16),
            pltpu.VMEM((C, REST, 128), BF16),
            pltpu.VMEM((G, A, REST, 128), BF16),
            pltpu.VMEM((A, N, 128), BF16),
            pltpu.VMEM((A, N, 128), BF16),
            pltpu.VMEM((C, K, 128), BF16),
            pltpu.VMEM((A, G, REST, 128), BF16),
            pltpu.VMEM((A, G, REST, 128), BF16),
            pltpu.VMEM((C, REST, 128), BF16),
            pltpu.VMEM((2, N, 128), BF16),
            pltpu.VMEM((2, N, 128), BF16),
            pltpu.VMEM((N, N), BF16),
            pltpu.SemaphoreType.DMA((7,)),
            pltpu.SemaphoreType.DMA((7,)),
        ],
        compiler_params=pltpu.CompilerParams(
            collective_id=0, has_side_effects=True, vmem_limit_bytes=58 * 2**20
        ),
        cost_estimate=pl.CostEstimate(
            flops=6_500_000_000, bytes_accessed=16_000_000, transcendentals=5_000_000
        ),
    )(
        pair_map,
        pair_mask,
        input_gain[None],
        input_bias[None],
        input_weights,
        output_gain[None],
        output_bias[None],
        output_weight,
    )
    return jnp.transpose(result, (1, 0, 2))


def solution(mesh):
    return jax.shard_map(
        per_device,
        mesh=mesh,
        in_specs=(
            P(("pr", "pc"), "grp", None),
            P(("pr", "pc"), "grp"),
            P(),
            P(),
            P(),
            P(),
            P(),
            P(),
        ),
        out_specs=P(("pr", "pc"), "grp", None),
        check_vma=False,
    )
```

```python
import jax
import jax.numpy as jnp
from jax import lax
from jax.experimental import pallas as pl
from jax.experimental.pallas import tpu as pltpu
from jax.sharding import PartitionSpec as P

MESH = pl.DeviceIdType.MESH
F32 = jnp.float32
BF16 = jnp.bfloat16
epsilon = 1e-05

I = 160
K = 80
C = 128
G = 16
A = 8
N = 1280
REST = 24
BOTH = 40
FIRST = 48
R_MAIN, BOTH_REST, L_MAIN, T_REST, T_FIRST, T_LAST = range(6)


def kernel(
    x_ref,
    mask_ref,
    gain_ref,
    bias_ref,
    weights_ref,
    ogain_ref,
    obias_ref,
    ow_ref,
    o_ref,
    wide,
    normed,
    gates,
    swap,
    proj,
    mask_main,
    mask_rest,
    scaling,
    out_l,
    out_r,
    out_t,
    out_rest,
    out_t_rest,
    in_l,
    in_r,
    in_t,
    in_rest,
    in_t_rest,
    rest_l,
    rest_r,
    right_t,
    send_sem,
    recv_sem,
):
    g = lax.axis_index("grp")
    y = lax.axis_index("pr")
    core = lax.axis_index("pc")
    x, z = g >> 2, g & 3
    a = y * 2 + core
    quarter = a & 3
    mine = g * A + a

    def partner(step):
        v = (step * 47) & 127
        w = v & 3
        px = (x + (w ^ (w >> 1))) & 3
        pcore = core ^ ((v >> 2) & 1)
        py = (y + (v >> 3)) & 3
        pz = (z + (v >> 5)) & 3
        return px * 4 + pz, py, pcore

    def place(pg, py, pcore):
        return {"grp": pg, "pr": py, "pc": pcore}

    barrier = pltpu.get_barrier_semaphore()

    def each_partner(visit):
        def several(n, carry):
            for u in range(7):
                visit(*partner(n * 7 + u + 1))
            return carry

        lax.fori_loop(0, 18, several, 0)
        visit(*partner(127))

    def greet(pg, py, pcore):
        pl.semaphore_signal(
            barrier, inc=1, device_id=place(pg, py, pcore), device_id_type=MESH
        )

    each_partner(greet)

    def by_group(parts):
        group = lax.broadcasted_iota(jnp.int32, parts[0].shape, 1) // 32
        return jnp.where(
            group == 0,
            parts[0],
            jnp.where(group == 1, parts[1], jnp.where(group == 2, parts[2], parts[3])),
        )

    def token(s, r, low):
        n = (quarter - s + 4) & 3
        return n * 16 + r if low else 64 + n * 4 + r

    def by_16(value):
        return pl.multiple_of(value, 16)

    for part in range(4):
        columns = weights_ref[:, part * C : (part + 1) * C].astype(F32)
        proj[part * C : (part + 1) * C, :] = columns.T.astype(BF16)
    scaling[0] = jnp.broadcast_to(ogain_ref[...], (C, 128)).T
    scaling[1] = jnp.broadcast_to(obias_ref[...], (C, 128)).T
    mask = mask_ref[...].astype(F32).T
    mask_main[...] = mask[:, :128]
    mask_rest[...] = jnp.concatenate([mask[:, 128:]] * 4, axis=1)
    ones = jnp.full((256, 128), 1 / 128, BF16)

    def normalize(b):
        def rows(i, carry):
            block = x_ref[pl.ds(i * 32, 32), pl.ds(by_16(b * 16), 16), :].reshape(512, C)
            center = jnp.dot(block, ones[:128], preferred_element_type=F32)
            shifted = block.astype(F32) - center
            squares = shifted * shifted
            high = squares.astype(BF16)
            low = (squares - high.astype(F32)).astype(BF16)
            spread = jnp.dot(
                jnp.concatenate([high, low], axis=1), ones, preferred_element_type=F32
            )
            wide[pl.ds(i * 512, 512), :] = (
                shifted * lax.rsqrt(spread + epsilon) * gain_ref[...] + bias_ref[...]
            )
            return carry

        lax.fori_loop(0, I // 32, rows, 0)

        def turn(k, carry):
            normed[b * 16 + k] = wide[pl.ds(k, I, stride=16), :].astype(BF16)
            return carry

        lax.fori_loop(0, 16, turn, 0, unroll=2)

    def gated(tokens, weights, mask_rows):
        both = lax.dot_general(
            weights, tokens, (((1,), (1,)), ((), ())), preferred_element_type=F32
        )
        value, gate = both[:C], both[C:]
        return value * jax.nn.sigmoid(gate) * mask_rows

    def project_main(k, at, first):
        tokens = normed[pl.ds(k, 2), 0:128, :].reshape(256, C)
        rows = mask_main[pl.ds(k, 2), :]
        result = gated(
            tokens, proj[first : first + 2 * C, :], jnp.concatenate([rows[0:1], rows[1:2]], axis=1)
        )
        swap[pl.ds(at * C, C), :] = result[:, :128]
        swap[pl.ds(at * C + C, C), :] = result[:, 128:]

    def rest_tokens(r, low):
        return jnp.concatenate([normed[token(s, r, low), 128:, :] for s in range(4)], axis=0)

    def rest_mask(r, low):
        return by_group([mask_rest[pl.ds(token(s, r, low), 1), :] for s in range(4)])

    def project_rest(r, at, low, first):
        tokens = jnp.concatenate([rest_tokens(r, low), rest_tokens(r + 1, low)], axis=0)
        result = gated(
            tokens,
            proj[first : first + 2 * C, :],
            jnp.concatenate([rest_mask(r, low), rest_mask(r + 1, low)], axis=1),
        )
        swap[pl.ds(at * C, C), :] = result[:, :128]
        swap[pl.ds(at * C + C, C), :] = result[:, 128:]

    def ready(c):
        return

    def send_round(prepare, source, target, which):
        def one(pg, py, pcore):
            pa = py * 2 + pcore
            prepare(pg * A + pa)
            pltpu.make_async_remote_copy(
                src_ref=source(pg, pa),
                dst_ref=target,
                send_sem=send_sem.at[which],
                recv_sem=recv_sem.at[which],
                device_id=place(pg, py, pcore),
                device_id_type=MESH,
            ).start()

        prepare(mine)
        pltpu.make_async_copy(source(g, a), target, recv_sem.at[which]).start()
        each_partner(one)

    def wait_all(buffer, semaphore):
        pltpu.make_async_copy(buffer, buffer, semaphore).wait()

    def send_main(start, rows, store, target, which):
        from_row = pl.ds(by_16(start), rows)

        def prepare(c):
            store[c, from_row, :] = swap[pl.ds(c, rows, stride=C), :].astype(BF16)

        send_round(
            prepare,
            lambda pg, pa: store.at[pg * A + pa, from_row],
            target.at[a, pl.ds(by_16(g * K + start), rows)],
            which,
        )

    def project_rows(start, count, first):
        def pair(p, carry):
            project_main(start + p * 2, p * 2, first)
            return carry

        lax.fori_loop(0, count // 2, pair, 0)

    normalize(0)
    project_rows(0, 16, 2 * C)
    pl.semaphore_wait(barrier, 127)
    send_main(0, 16, out_r, in_r, R_MAIN)

    def right_block(b, carry):
        normalize(2 * b + 1)
        normalize(2 * b + 2)
        start = 32 * b + 16
        project_rows(start, 32, 2 * C)
        send_main(start, 32, out_r, in_r, R_MAIN)
        return carry

    lax.fori_loop(0, 2, right_block, 0)

    def low_rest(p, carry):
        project_rest(p * 2, p * 2, True, 2 * C)
        project_rest(p * 2, 16 + p * 2, True, 0)
        return carry

    lax.fori_loop(0, 8, low_rest, 0)

    def high_rest(p, carry):
        project_rest(p * 2, 32 + p * 2, False, 2 * C)
        project_rest(p * 2, 36 + p * 2, False, 0)
        return carry

    lax.fori_loop(0, 2, high_rest, 0)

    def prepare_rest(c):
        out_rest[c] = swap[pl.ds(c, BOTH, stride=C), :].astype(BF16)

    send_round(
        prepare_rest, lambda pg, pa: out_rest.at[pg * A + pa], in_rest.at[a, g], BOTH_REST
    )

    for start, count in ((0, 32), (32, 48)):
        project_rows(start, count, 0)
        send_main(start, count, out_l, in_l, L_MAIN)

    def open_gate(p, carry):
        tokens = normed[pl.ds(p * 2, 2)].reshape(2 * I, C)
        gates[pl.ds(p * 2, 2)] = jax.nn.sigmoid(
            jnp.dot(tokens, weights_ref[:, 4 * C :], preferred_element_type=F32)
        ).reshape(2, I, C)
        return carry

    lax.fori_loop(0, K // 2, open_gate, 0)

    def spread_rest(side, rest):
        def one(step, carry):
            h, sg = step >> 4, step & 15
            parts = [
                in_rest[4 * h + t, sg, 16 * side : 16 * side + 16, :].astype(F32) for t in range(4)
            ]
            tails = [in_rest[4 * h + t, sg, 32:40, :].astype(F32) for t in range(4)]
            if side:
                tails = [pltpu.roll(tail, 4, 0) for tail in tails]
            at = sg * K
            ends = []
            for n in range(4):
                rows = by_group([parts[(s + n) % 4] for s in range(4)])
                tail = by_group([tails[(s + n) % 4] for s in range(4)])
                if n:
                    rows = pltpu.roll(rows, 32 * n, 1)
                    tail = pltpu.roll(tail, 32 * n, 1)
                rest[h, pl.ds(by_16(at + n * 16), 16), :] = rows.astype(BF16)
                ends.append(tail)
            upper = lax.broadcasted_iota(jnp.int32, (8, 128), 0) < 4
            joined = jnp.concatenate(
                [
                    jnp.where(upper, ends[0], pltpu.roll(ends[1], 4, 0)),
                    jnp.where(upper, ends[2], pltpu.roll(ends[3], 4, 0)),
                ],
                axis=0,
            )
            rest[h, pl.ds(by_16(at + 64), 16), :] = joined.astype(BF16)
            return carry

        lax.fori_loop(0, 2 * G, one, 0)

    wait_all(in_r, recv_sem.at[R_MAIN])

    def turn_main(b, carry):
        right_t[pl.ds(pl.multiple_of(b * I, 32), 128), :] = in_r[b].T
        return carry

    lax.fori_loop(0, A, turn_main, 0)

    wait_all(in_rest, recv_sem.at[BOTH_REST])
    spread_rest(0, rest_r)

    def turn_rest(h, carry):
        turned = rest_r[h].T
        for t in range(4):
            right_t[pl.ds(pl.multiple_of((4 * h + t) * I + 128, 32), 32), :] = turned[
                32 * t : 32 * t + 32
            ]
        return carry

    lax.fori_loop(0, 2, turn_rest, 0)

    spread_rest(1, rest_l)

    def rest_product(m, carry):
        rows = right_t[pl.ds(pl.multiple_of(m * 320, 32), 320), :]
        columns = jnp.concatenate([rest_l[0], rest_l[1]], axis=1)
        product = jnp.dot(rows, columns, preferred_element_type=F32)
        for h in range(2):
            for sg in range(4):
                block = product[sg * K : (sg + 1) * K, h * 128 : (h + 1) * 128]
                mains, tails = [], []
                for n in range(4):
                    main = block[n * 16 : (n + 1) * 16]
                    tail = block[64 + 8 * (n // 2) : 72 + 8 * (n // 2)]
                    if n % 2:
                        tail = pltpu.roll(tail, 4, 0)
                    if n:
                        main = pltpu.roll(main, 128 - 32 * n, 1)
                        tail = pltpu.roll(tail, 128 - 32 * n, 1)
                    mains.append(main)
                    tails.append(tail)
                for t in range(4):
                    out_t_rest[m * 4 + sg, 4 * h + t, 0:16, :] = by_group(
                        [mains[(t - s) % 4] for s in range(4)]
                    ).astype(BF16)
                    out_t_rest[m * 4 + sg, 4 * h + t, 16:24, :] = by_group(
                        [tails[(t - s) % 4] for s in range(4)]
                    ).astype(BF16)
        return carry

    lax.fori_loop(0, 4, rest_product, 0)
    send_round(ready, lambda pg, pa: out_t_rest.at[pg, pa], in_t_rest.at[mine], T_REST)

    wait_all(in_l, recv_sem.at[L_MAIN])

    def main_product(step, carry):
        i, j = step & 3, step >> 2
        dx = (1 + 2 * i + (i >> 1)) & 3
        dy = (3 * dx + j) & 3
        tx, ty = (x + dx) & 3, (y + dy) & 3
        rows = right_t[pl.ds(pl.multiple_of(tx * 320, 32), 320), :]
        columns = jnp.concatenate([in_l[2 * ty], in_l[2 * ty + 1]], axis=1)
        product = jnp.dot(rows, columns, preferred_element_type=F32).astype(BF16)
        for h in range(2):
            out_t[pl.ds(tx * 4, 4), 2 * ty + h] = product[
                :, h * 128 : (h + 1) * 128
            ].reshape(4, K, 128)

        def send(q, carry):
            pg, pcore = tx * 4 + ((z + (q >> 1)) & 3), core ^ (q & 1)
            source = out_t.at[pg, 2 * ty + pcore, pl.ds(0, FIRST)]
            target = in_t.at[mine, pl.ds(0, FIRST)]
            own = (dx == 0) & (dy == 0) & (q == 0)

            @pl.when(own)
            def _():
                pltpu.make_async_copy(source, target, recv_sem.at[T_FIRST]).start()

            @pl.when(jnp.logical_not(own))
            def _():
                pltpu.make_async_remote_copy(
                    src_ref=source,
                    dst_ref=target,
                    send_sem=send_sem.at[T_FIRST],
                    recv_sem=recv_sem.at[T_FIRST],
                    device_id=place(pg, ty, pcore),
                    device_id_type=MESH,
                ).start()

            return carry

        lax.fori_loop(0, 8, send, 0)
        return carry

    lax.fori_loop(0, 16, main_product, 0)
    last = pl.ds(FIRST, K - FIRST)
    send_round(ready, lambda pg, pa: out_t.at[pg, pa, last], in_t.at[mine, last], T_LAST)

    def settle(r, rows):
        values = swap[pl.ds(r, C, stride=rows), :]
        center = jnp.mean(values, axis=0, keepdims=True)
        shifted = values - center
        spread = jnp.mean(shifted * shifted, axis=0, keepdims=True)
        settled = (shifted * lax.rsqrt(spread + epsilon) * scaling[0] + scaling[1]).astype(BF16)
        return lax.dot_general(
            settled, ow_ref[...], (((0,), (0,)), ((), ())), preferred_element_type=F32
        )

    def widen(arrived, at, rows):
        def one(c, carry):
            swap[pl.ds(pl.multiple_of(c * rows, 8), rows), :] = arrived[
                c, pl.ds(at, rows), :
            ].astype(F32)
            return carry

        lax.fori_loop(0, C, one, 0, unroll=8)

    def finish(b, carry):
        widen(in_t, by_16(b * 16), 16)

        def one(r, carry):
            j = b * 16 + r
            o_ref[j, 0:128, :] = (gates[j, 0:128, :] * settle(r, 16)).astype(BF16)
            return carry

        lax.fori_loop(0, 16, one, 0, unroll=4)
        return carry

    wait_all(in_t_rest, recv_sem.at[T_REST])
    for low, count, rows, at in ((True, 16, 16, 0), (False, 4, 8, 16)):
        widen(in_t_rest, at, rows)

        def one_rest(r, carry):
            mixed = settle(r, rows)
            for s in range(4):
                j = token(s, r, low)
                o_ref[j, 128:, :] = (
                    gates[j, 128:, :] * mixed[32 * s : 32 * s + 32]
                ).astype(BF16)
            return carry

        lax.fori_loop(0, count, one_rest, 0, unroll=4)

    wait_all(in_t.at[:, pl.ds(0, FIRST)], recv_sem.at[T_FIRST])
    lax.fori_loop(0, FIRST // 16, finish, 0)
    wait_all(in_t.at[:, last], recv_sem.at[T_LAST])
    lax.fori_loop(FIRST // 16, K // 16, finish, 0)

    for which, buffer in (
        (R_MAIN, out_r),
        (BOTH_REST, out_rest),
        (L_MAIN, out_l),
        (T_REST, in_t_rest),
        (T_FIRST, in_t.at[:, pl.ds(0, FIRST)]),
        (T_LAST, in_t.at[:, last]),
    ):
        wait_all(buffer.at[pl.ds(0, 127)], send_sem.at[which])


def per_device(
    pair_map,
    pair_mask,
    input_gain,
    input_bias,
    input_weights,
    output_gain,
    output_bias,
    output_weight,
):
    vmem = pl.BlockSpec(memory_space=pltpu.VMEM)
    result = pl.pallas_call(
        kernel,
        out_shape=jax.ShapeDtypeStruct((K, I, C), BF16),
        in_specs=[vmem] * 8,
        out_specs=vmem,
        scratch_shapes=[
            pltpu.VMEM((I * 16, C), F32),
            pltpu.VMEM((K, I, C), BF16),
            pltpu.VMEM((K, I, C), F32),
            pltpu.VMEM((48 * C, 128), F32),
            pltpu.VMEM((4 * C, C), BF16),
            pltpu.VMEM((K, 128), F32),
            pltpu.VMEM((K, 128), F32),
            pltpu.VMEM((2, C, 128), F32),
            pltpu.VMEM((C, K, 128), BF16),
            pltpu.VMEM((C, K, 128), BF16),
            pltpu.VMEM((G, A, K, 128), BF16),
            pltpu.VMEM((C, BOTH, 128), BF16),
            pltpu.VMEM((G, A, REST, 128), BF16),
            pltpu.VMEM((A, N, 128), BF16),
            pltpu.VMEM((A, N, 128), BF16),
            pltpu.VMEM((C, K, 128), BF16),
            pltpu.VMEM((A, G, BOTH, 128), BF16),
            pltpu.VMEM((C, REST, 128), BF16),
            pltpu.VMEM((2, N, 128), BF16),
            pltpu.VMEM((2, N, 128), BF16),
            pltpu.VMEM((N, N), BF16),
            pltpu.SemaphoreType.DMA((6,)),
            pltpu.SemaphoreType.DMA((6,)),
        ],
        compiler_params=pltpu.CompilerParams(
            collective_id=0, has_side_effects=True, vmem_limit_bytes=58 * 2**20
        ),
        cost_estimate=pl.CostEstimate(
            flops=6_500_000_000, bytes_accessed=16_000_000, transcendentals=5_000_000
        ),
    )(
        pair_map,
        pair_mask,
        input_gain[None],
        input_bias[None],
        input_weights,
        output_gain[None],
        output_bias[None],
        output_weight,
    )
    return jnp.transpose(result, (1, 0, 2))


def solution(mesh):
    return jax.shard_map(
        per_device,
        mesh=mesh,
        in_specs=(
            P(("pr", "pc"), "grp", None),
            P(("pr", "pc"), "grp"),
            P(),
            P(),
            P(),
            P(),
            P(),
            P(),
        ),
        out_specs=P(("pr", "pc"), "grp", None),
        check_vma=False,
    )
```

```python
import jax
import jax.numpy as jnp
from jax import lax
from jax.experimental import pallas as pl
from jax.experimental.pallas import tpu as pltpu
from jax.sharding import PartitionSpec as P

MESH = pl.DeviceIdType.MESH
F32 = jnp.float32
BF16 = jnp.bfloat16
epsilon = 1e-05

I = 160
K = 80
C = 128
G = 16
A = 8
N = 1280
REST = 24
BOTH = 40
FIRST = 64
R_MAIN, BOTH_REST, L_MAIN, T_REST, T_FIRST, T_LAST = range(6)


def kernel(
    x_hbm,
    mask_ref,
    gain_ref,
    bias_ref,
    weights_ref,
    ogain_ref,
    obias_ref,
    ow_ref,
    o_hbm,
    x_ref,
    o_ref,
    wide,
    normed,
    gates,
    swap,
    proj,
    gate_weights,
    mask_main,
    mask_rest,
    scaling,
    out_l,
    out_r,
    out_t,
    out_rest,
    out_t_rest,
    in_l,
    in_r,
    in_t,
    in_rest,
    in_t_rest,
    rest_l,
    rest_r,
    right_t,
    fetch_sem,
    store_sem,
    entry_sem,
    send_sem,
    recv_sem,
):
    g = lax.axis_index("grp")
    y = lax.axis_index("pr")
    core = lax.axis_index("pc")
    x, z = g >> 2, g & 3
    a = y * 2 + core
    quarter = a & 3
    mine = g * A + a

    def partner(step):
        v = (step * 47) & 127
        w = v & 3
        px = (x + (w ^ (w >> 1))) & 3
        pcore = core ^ ((v >> 2) & 1)
        py = (y + (v >> 3)) & 3
        pz = (z + (v >> 5)) & 3
        return px * 4 + pz, py, pcore

    def place(pg, py, pcore):
        return {"grp": pg, "pr": py, "pc": pcore}

    barrier = pltpu.get_barrier_semaphore()

    def each_partner(visit):
        def several(n, carry):
            for u in range(7):
                visit(*partner(n * 7 + u + 1))
            return carry

        lax.fori_loop(0, 18, several, 0)
        visit(*partner(127))

    def greet_row(semaphore):
        for step in range(1, A):
            pl.semaphore_signal(
                semaphore,
                inc=1,
                device_id=place(g, (y + (step >> 1)) & 3, core ^ (step & 1)),
                device_id_type=MESH,
            )

    def greet_column(step, carry):
        pl.semaphore_signal(
            barrier, inc=1, device_id=place((g + step) & 15, y, core), device_id_type=MESH
        )
        return carry

    lax.fori_loop(1, G, greet_column, 0, unroll=5)
    greet_row(barrier)

    def fetch(b):
        block = pl.ds(b * 16, 16)
        return pltpu.make_async_copy(x_hbm.at[:, block], x_ref.at[:, block], fetch_sem.at[b])

    for b in range(5):
        fetch(b).start()

    def by_group(parts):
        group = lax.broadcasted_iota(jnp.int32, parts[0].shape, 1) // 32
        return jnp.where(
            group == 0,
            parts[0],
            jnp.where(group == 1, parts[1], jnp.where(group == 2, parts[2], parts[3])),
        )

    def token(s, r, low):
        n = (quarter - s + 4) & 3
        return n * 16 + r if low else 64 + n * 4 + r

    def by_16(value):
        return pl.multiple_of(value, 16)

    for part in range(4):
        columns = weights_ref[:, part * C : (part + 1) * C].astype(F32)
        proj[part * C : (part + 1) * C, :] = (0.5 * columns.T).astype(BF16)
    gate_weights[...] = (0.5 * weights_ref[:, 4 * C :].astype(F32)).astype(BF16)
    scaling[0] = jnp.broadcast_to(ogain_ref[...], (C, 128)).T
    scaling[1] = jnp.broadcast_to(obias_ref[...], (C, 128)).T
    mask = mask_ref[...].astype(F32).T
    mask_main[...] = mask[:, :128]
    mask_rest[...] = jnp.concatenate([mask[:, 128:]] * 4, axis=1)
    ones = jnp.full((256, 128), 1 / 128, BF16)

    def normalize(b):
        def rows(i, carry):
            block = x_ref[pl.ds(i * 32, 32), pl.ds(by_16(b * 16), 16), :].reshape(512, C)
            center = jnp.dot(block, ones[:128], preferred_element_type=F32)
            shifted = block.astype(F32) - center
            squares = shifted * shifted
            high = squares.astype(BF16)
            low = (squares - high.astype(F32)).astype(BF16)
            spread = jnp.dot(
                jnp.concatenate([high, low], axis=1), ones, preferred_element_type=F32
            )
            wide[pl.ds(i * 512, 512), :] = (
                shifted * lax.rsqrt(spread + epsilon) * gain_ref[...] + bias_ref[...]
            )
            return carry

        lax.fori_loop(0, I // 32, rows, 0)

        def turn(k, carry):
            normed[b * 16 + k] = wide[pl.ds(k, I, stride=16), :].astype(BF16)
            return carry

        lax.fori_loop(0, 16, turn, 0, unroll=2)

    def gated(tokens, weights, mask_rows):
        both = lax.dot_general(
            weights, tokens, (((1,), (1,)), ((), ())), preferred_element_type=F32
        )
        half_value, half_gate = both[:C], both[C:]
        return (half_value + half_value * jnp.tanh(half_gate)) * mask_rows

    def project_main(k, at, first):
        tokens = normed[pl.ds(k, 2), 0:128, :].reshape(256, C)
        rows = mask_main[pl.ds(k, 2), :]
        result = gated(
            tokens, proj[first : first + 2 * C, :], jnp.concatenate([rows[0:1], rows[1:2]], axis=1)
        )
        swap[pl.ds(at * C, C), :] = result[:, :128]
        swap[pl.ds(at * C + C, C), :] = result[:, 128:]

    def rest_tokens(r, low):
        return jnp.concatenate([normed[token(s, r, low), 128:, :] for s in range(4)], axis=0)

    def rest_mask(r, low):
        return by_group([mask_rest[pl.ds(token(s, r, low), 1), :] for s in range(4)])

    def project_rest(r, at, low, first):
        tokens = jnp.concatenate([rest_tokens(r, low), rest_tokens(r + 1, low)], axis=0)
        result = gated(
            tokens,
            proj[first : first + 2 * C, :],
            jnp.concatenate([rest_mask(r, low), rest_mask(r + 1, low)], axis=1),
        )
        swap[pl.ds(at * C, C), :] = result[:, :128]
        swap[pl.ds(at * C + C, C), :] = result[:, 128:]

    def ready(c):
        return

    def send_round(prepare, source, target, which):
        def one(pg, py, pcore):
            pa = py * 2 + pcore
            prepare(pg * A + pa)
            pltpu.make_async_remote_copy(
                src_ref=source(pg, pa),
                dst_ref=target,
                send_sem=send_sem.at[which],
                recv_sem=recv_sem.at[which],
                device_id=place(pg, py, pcore),
                device_id_type=MESH,
            ).start()

        prepare(mine)
        pltpu.make_async_copy(source(g, a), target, recv_sem.at[which]).start()
        each_partner(one)

    def wait_all(buffer, semaphore):
        pltpu.make_async_copy(buffer, buffer, semaphore).wait()

    def send_main(start, rows, store, target, which):
        from_row = pl.ds(by_16(start), rows)

        def prepare(c):
            store[c, from_row, :] = swap[pl.ds(c, rows, stride=C), :].astype(BF16)

        send_round(
            prepare,
            lambda pg, pa: store.at[pg * A + pa, from_row],
            target.at[a, pl.ds(by_16(g * K + start), rows)],
            which,
        )

    def project_rows(start, count, first):
        def pair(p, carry):
            project_main(start + p * 2, p * 2, first)
            return carry

        lax.fori_loop(0, count // 2, pair, 0)

    def left_rows(start, count):
        project_rows(start, count, 0)
        send_main(start, count, out_l, in_l, L_MAIN)

    def right_rows(start, count):
        project_rows(start, count, 2 * C)
        send_main(start, count, out_r, in_r, R_MAIN)

    fetch(0).wait()
    normalize(0)
    pl.semaphore_wait(barrier, G + A - 2)
    greet_row(entry_sem)
    project_rows(0, 16, 2 * C)
    pl.semaphore_wait(entry_sem, A - 1)
    send_main(0, 16, out_r, in_r, R_MAIN)
    left_rows(0, 16)
    for b in range(2):
        fetch(2 * b + 1).wait()
        normalize(2 * b + 1)
        fetch(2 * b + 2).wait()
        normalize(2 * b + 2)
        right_rows(32 * b + 16, 32)

    def low_rest(p, carry):
        project_rest(p * 2, p * 2, True, 2 * C)
        project_rest(p * 2, 16 + p * 2, True, 0)
        return carry

    lax.fori_loop(0, 8, low_rest, 0)

    def high_rest(p, carry):
        project_rest(p * 2, 32 + p * 2, False, 2 * C)
        project_rest(p * 2, 36 + p * 2, False, 0)
        return carry

    lax.fori_loop(0, 2, high_rest, 0)

    def prepare_rest(c):
        out_rest[c] = swap[pl.ds(c, BOTH, stride=C), :].astype(BF16)

    send_round(
        prepare_rest, lambda pg, pa: out_rest.at[pg * A + pa], in_rest.at[a, g], BOTH_REST
    )

    left_rows(16, 32)
    left_rows(48, 32)

    def open_gate(p, carry):
        tokens = normed[pl.ds(p * 2, 2)].reshape(2 * I, C)
        half = jnp.dot(tokens, gate_weights[...], preferred_element_type=F32)
        gates[pl.ds(p * 2, 2)] = (0.5 + 0.5 * jnp.tanh(half)).reshape(2, I, C)
        return carry

    lax.fori_loop(0, K // 2, open_gate, 0)

    def spread_rest(side, rest):
        def one(step, carry):
            h, sg = step >> 4, step & 15
            parts = [
                in_rest[4 * h + t, sg, 16 * side : 16 * side + 16, :].astype(F32) for t in range(4)
            ]
            tails = [in_rest[4 * h + t, sg, 32:40, :].astype(F32) for t in range(4)]
            if side:
                tails = [pltpu.roll(tail, 4, 0) for tail in tails]
            at = sg * K
            ends = []
            for n in range(4):
                rows = by_group([parts[(s + n) % 4] for s in range(4)])
                tail = by_group([tails[(s + n) % 4] for s in range(4)])
                if n:
                    rows = pltpu.roll(rows, 32 * n, 1)
                    tail = pltpu.roll(tail, 32 * n, 1)
                rest[h, pl.ds(by_16(at + n * 16), 16), :] = rows.astype(BF16)
                ends.append(tail)
            upper = lax.broadcasted_iota(jnp.int32, (8, 128), 0) < 4
            joined = jnp.concatenate(
                [
                    jnp.where(upper, ends[0], pltpu.roll(ends[1], 4, 0)),
                    jnp.where(upper, ends[2], pltpu.roll(ends[3], 4, 0)),
                ],
                axis=0,
            )
            rest[h, pl.ds(by_16(at + 64), 16), :] = joined.astype(BF16)
            return carry

        lax.fori_loop(0, 2 * G, one, 0)

    wait_all(in_r, recv_sem.at[R_MAIN])

    def turn_main(b, carry):
        right_t[pl.ds(pl.multiple_of(b * I, 32), 128), :] = in_r[b].T
        return carry

    lax.fori_loop(0, A, turn_main, 0)

    wait_all(in_rest, recv_sem.at[BOTH_REST])
    spread_rest(0, rest_r)

    def turn_rest(h, carry):
        turned = rest_r[h].T
        for t in range(4):
            right_t[pl.ds(pl.multiple_of((4 * h + t) * I + 128, 32), 32), :] = turned[
                32 * t : 32 * t + 32
            ]
        return carry

    lax.fori_loop(0, 2, turn_rest, 0)

    spread_rest(1, rest_l)

    def rest_product(m, carry):
        rows = right_t[pl.ds(pl.multiple_of(m * 320, 32), 320), :]
        columns = jnp.concatenate([rest_l[0], rest_l[1]], axis=1)
        product = jnp.dot(rows, columns, preferred_element_type=F32)
        for h in range(2):
            for sg in range(4):
                block = product[sg * K : (sg + 1) * K, h * 128 : (h + 1) * 128]
                mains, tails = [], []
                for n in range(4):
                    main = block[n * 16 : (n + 1) * 16]
                    tail = block[64 + 8 * (n // 2) : 72 + 8 * (n // 2)]
                    if n % 2:
                        tail = pltpu.roll(tail, 4, 0)
                    if n:
                        main = pltpu.roll(main, 128 - 32 * n, 1)
                        tail = pltpu.roll(tail, 128 - 32 * n, 1)
                    mains.append(main)
                    tails.append(tail)
                for t in range(4):
                    out_t_rest[m * 4 + sg, 4 * h + t, 0:16, :] = by_group(
                        [mains[(t - s) % 4] for s in range(4)]
                    ).astype(BF16)
                    out_t_rest[m * 4 + sg, 4 * h + t, 16:24, :] = by_group(
                        [tails[(t - s) % 4] for s in range(4)]
                    ).astype(BF16)
        return carry

    lax.fori_loop(0, 4, rest_product, 0)
    send_round(ready, lambda pg, pa: out_t_rest.at[pg, pa], in_t_rest.at[mine], T_REST)

    wait_all(in_l, recv_sem.at[L_MAIN])

    def main_product(step, carry):
        i, j = step & 3, step >> 2
        dx = (1 + 2 * i + (i >> 1)) & 3
        dy = (3 * dx + j) & 3
        tx, ty = (x + dx) & 3, (y + dy) & 3
        rows = right_t[pl.ds(pl.multiple_of(tx * 320, 32), 320), :]
        columns = jnp.concatenate([in_l[2 * ty], in_l[2 * ty + 1]], axis=1)
        product = jnp.dot(rows, columns, preferred_element_type=F32).astype(BF16)
        for h in range(2):
            out_t[pl.ds(tx * 4, 4), 2 * ty + h] = product[
                :, h * 128 : (h + 1) * 128
            ].reshape(4, K, 128)

        def send(q, carry):
            pg, pcore = tx * 4 + ((z + (q >> 1)) & 3), core ^ (q & 1)
            source = out_t.at[pg, 2 * ty + pcore, pl.ds(0, FIRST)]
            target = in_t.at[mine, pl.ds(0, FIRST)]
            own = (dx == 0) & (dy == 0) & (q == 0)

            @pl.when(own)
            def _():
                pltpu.make_async_copy(source, target, recv_sem.at[T_FIRST]).start()

            @pl.when(jnp.logical_not(own))
            def _():
                pltpu.make_async_remote_copy(
                    src_ref=source,
                    dst_ref=target,
                    send_sem=send_sem.at[T_FIRST],
                    recv_sem=recv_sem.at[T_FIRST],
                    device_id=place(pg, ty, pcore),
                    device_id_type=MESH,
                ).start()

            return carry

        lax.fori_loop(0, 8, send, 0)
        return carry

    lax.fori_loop(0, 16, main_product, 0)
    last = pl.ds(FIRST, K - FIRST)
    send_round(ready, lambda pg, pa: out_t.at[pg, pa, last], in_t.at[mine, last], T_LAST)

    def settle(r, rows):
        values = swap[pl.ds(r, C, stride=rows), :]
        center = jnp.mean(values, axis=0, keepdims=True)
        shifted = values - center
        spread = jnp.mean(shifted * shifted, axis=0, keepdims=True)
        settled = (shifted * lax.rsqrt(spread + epsilon) * scaling[0] + scaling[1]).astype(BF16)
        return lax.dot_general(
            settled, ow_ref[...], (((0,), (0,)), ((), ())), preferred_element_type=F32
        )

    def widen(arrived, at, rows):
        def one(c, carry):
            swap[pl.ds(pl.multiple_of(c * rows, 8), rows), :] = arrived[
                c, pl.ds(at, rows), :
            ].astype(F32)
            return carry

        lax.fori_loop(0, C, one, 0, unroll=8)

    def finish(b, carry):
        widen(in_t, by_16(b * 16), 16)

        def one(r, carry):
            j = b * 16 + r
            o_ref[j, 0:128, :] = (gates[j, 0:128, :] * settle(r, 16)).astype(BF16)
            return carry

        lax.fori_loop(0, 16, one, 0, unroll=4)
        return carry

    wait_all(in_t_rest, recv_sem.at[T_REST])
    for low, count, rows, at in ((True, 16, 16, 0), (False, 4, 8, 16)):
        widen(in_t_rest, at, rows)

        def one_rest(r, carry):
            mixed = settle(r, rows)
            for s in range(4):
                j = token(s, r, low)
                o_ref[j, 128:, :] = (
                    gates[j, 128:, :] * mixed[32 * s : 32 * s + 32]
                ).astype(BF16)
            return carry

        lax.fori_loop(0, count, one_rest, 0, unroll=4)

    wait_all(in_t.at[:, pl.ds(0, FIRST)], recv_sem.at[T_FIRST])
    lax.fori_loop(0, FIRST // 16, finish, 0)

    def put(number, block):
        return pltpu.make_async_copy(o_ref.at[block], o_hbm.at[block], store_sem.at[number])

    put(0, pl.ds(0, FIRST)).start()
    wait_all(in_t.at[:, last], recv_sem.at[T_LAST])
    lax.fori_loop(FIRST // 16, K // 16, finish, 0)
    put(1, last).start()

    for which, buffer in (
        (R_MAIN, out_r),
        (BOTH_REST, out_rest),
        (L_MAIN, out_l),
        (T_REST, in_t_rest),
        (T_FIRST, in_t.at[:, pl.ds(0, FIRST)]),
        (T_LAST, in_t.at[:, last]),
    ):
        wait_all(buffer.at[pl.ds(0, 127)], send_sem.at[which])
    put(0, pl.ds(0, FIRST)).wait()
    put(1, last).wait()


def per_device(
    pair_map,
    pair_mask,
    input_gain,
    input_bias,
    input_weights,
    output_gain,
    output_bias,
    output_weight,
):
    vmem = pl.BlockSpec(memory_space=pltpu.VMEM)
    result = pl.pallas_call(
        kernel,
        out_shape=jax.ShapeDtypeStruct((K, I, C), BF16),
        in_specs=[pl.BlockSpec(memory_space=pl.ANY)] + [vmem] * 7,
        out_specs=pl.BlockSpec(memory_space=pl.ANY),
        scratch_shapes=[
            pltpu.VMEM((I, K, C), BF16),
            pltpu.VMEM((K, I, C), BF16),
            pltpu.VMEM((I * 16, C), F32),
            pltpu.VMEM((K, I, C), BF16),
            pltpu.VMEM((K, I, C), F32),
            pltpu.VMEM((48 * C, 128), F32),
            pltpu.VMEM((4 * C, C), BF16),
            pltpu.VMEM((C, C), BF16),
            pltpu.VMEM((K, 128), F32),
            pltpu.VMEM((K, 128), F32),
            pltpu.VMEM((2, C, 128), F32),
            pltpu.VMEM((C, K, 128), BF16),
            pltpu.VMEM((C, K, 128), BF16),
            pltpu.VMEM((G, A, K, 128), BF16),
            pltpu.VMEM((C, BOTH, 128), BF16),
            pltpu.VMEM((G, A, REST, 128), BF16),
            pltpu.VMEM((A, N, 128), BF16),
            pltpu.VMEM((A, N, 128), BF16),
            pltpu.VMEM((C, K, 128), BF16),
            pltpu.VMEM((A, G, BOTH, 128), BF16),
            pltpu.VMEM((C, REST, 128), BF16),
            pltpu.VMEM((2, N, 128), BF16),
            pltpu.VMEM((2, N, 128), BF16),
            pltpu.VMEM((N, N), BF16),
            pltpu.SemaphoreType.DMA((5,)),
            pltpu.SemaphoreType.DMA((2,)),
            pltpu.SemaphoreType.REGULAR,
            pltpu.SemaphoreType.DMA((6,)),
            pltpu.SemaphoreType.DMA((6,)),
        ],
        compiler_params=pltpu.CompilerParams(
            collective_id=0, has_side_effects=True, vmem_limit_bytes=58 * 2**20
        ),
        cost_estimate=pl.CostEstimate(
            flops=6_500_000_000, bytes_accessed=16_000_000, transcendentals=5_000_000
        ),
    )(
        pair_map,
        pair_mask,
        input_gain[None],
        input_bias[None],
        input_weights,
        output_gain[None],
        output_bias[None],
        output_weight,
    )
    return jnp.transpose(result, (1, 0, 2))


def solution(mesh):
    return jax.shard_map(
        per_device,
        mesh=mesh,
        in_specs=(
            P(("pr", "pc"), "grp", None),
            P(("pr", "pc"), "grp"),
            P(),
            P(),
            P(),
            P(),
            P(),
            P(),
        ),
        out_specs=P(("pr", "pc"), "grp", None),
        check_vma=False,
    )
```

```python
import jax
import jax.numpy as jnp
from jax import lax
from jax.experimental import pallas as pl
from jax.experimental.pallas import tpu as pltpu
from jax.sharding import PartitionSpec as P

MESH = pl.DeviceIdType.MESH
F32 = jnp.float32
BF16 = jnp.bfloat16
epsilon = 1e-05

I = 160
K = 80
C = 128
G = 16
A = 8
N = 1280
PIECES = 8
REST = 24
BOTH = 40
FIRST = 48
R_MAIN, BOTH_REST, L_MAIN, T_REST, T_FIRST, T_NEXT, T_LAST = range(7)


def kernel(
    x_hbm,
    mask_ref,
    gain_ref,
    bias_ref,
    weights_ref,
    ogain_ref,
    obias_ref,
    ow_ref,
    o_hbm,
    x_ref,
    o_ref,
    late,
    wide,
    normed,
    gates,
    swap,
    proj,
    gate_weights,
    mask_main,
    mask_rest,
    scaling,
    out_l,
    out_r,
    out_t,
    out_rest,
    out_t_rest,
    in_l,
    in_r,
    in_t,
    in_rest,
    in_t_rest,
    rest_l,
    rest_r,
    right_t,
    fetch_sem,
    store_sem,
    entry_sem,
    send_sem,
    recv_sem,
):
    g = lax.axis_index("grp")
    y = lax.axis_index("pr")
    core = lax.axis_index("pc")
    x, z = g >> 2, g & 3
    a = y * 2 + core
    quarter = a & 3
    mine = g * A + a

    def partner(step):
        v = (step * 47) & 127
        w = v & 3
        px = (x + (w ^ (w >> 1))) & 3
        pcore = core ^ ((v >> 2) & 1)
        py = (y + (v >> 3)) & 3
        pz = (z + (v >> 5)) & 3
        return px * 4 + pz, py, pcore

    def place(pg, py, pcore):
        return {"grp": pg, "pr": py, "pc": pcore}

    barrier = pltpu.get_barrier_semaphore()

    def each_partner(visit):
        def several(n, carry):
            for u in range(7):
                visit(*partner(n * 7 + u + 1))
            return carry

        lax.fori_loop(0, 18, several, 0)
        visit(*partner(127))

    def greet_row(semaphore):
        for step in range(1, A):
            pl.semaphore_signal(
                semaphore,
                inc=1,
                device_id=place(g, (y + (step >> 1)) & 3, core ^ (step & 1)),
                device_id_type=MESH,
            )

    def greet_column(step, carry):
        pl.semaphore_signal(
            barrier, inc=1, device_id=place((g + step) & 15, y, core), device_id_type=MESH
        )
        return carry

    lax.fori_loop(1, G, greet_column, 0, unroll=5)
    greet_row(barrier)

    def fetch(b):
        block = pl.ds(b * 16, 16)
        return pltpu.make_async_copy(x_hbm.at[:, block], x_ref.at[:, block], fetch_sem.at[b])

    for b in range(5):
        fetch(b).start()

    def by_group(parts):
        group = lax.broadcasted_iota(jnp.int32, parts[0].shape, 1) // 32
        return jnp.where(
            group == 0,
            parts[0],
            jnp.where(group == 1, parts[1], jnp.where(group == 2, parts[2], parts[3])),
        )

    def token(s, r, low):
        n = (quarter - s + 4) & 3
        return n * 16 + r if low else 64 + n * 4 + r

    def by_16(value):
        return pl.multiple_of(value, 16)

    for part in range(4):
        columns = weights_ref[:, part * C : (part + 1) * C].astype(F32)
        proj[part * C : (part + 1) * C, :] = (0.5 * columns.T).astype(BF16)
    gate_weights[...] = (0.5 * weights_ref[:, 4 * C :].astype(F32)).astype(BF16)
    scaling[0] = jnp.broadcast_to(ogain_ref[...], (C, 128)).T
    scaling[1] = jnp.broadcast_to(obias_ref[...], (C, 128)).T
    mask = mask_ref[...].astype(F32).T
    mask_main[...] = mask[:, :128]
    mask_rest[...] = jnp.concatenate([mask[:, 128:]] * 4, axis=1)
    ones = jnp.full((256, 128), 1 / 128, BF16)

    def normalize(b):
        def rows(i, carry):
            block = x_ref[pl.ds(i * 32, 32), pl.ds(by_16(b * 16), 16), :].reshape(512, C)
            center = jnp.dot(block, ones[:128], preferred_element_type=F32)
            shifted = block.astype(F32) - center
            squares = shifted * shifted
            high = squares.astype(BF16)
            low = (squares - high.astype(F32)).astype(BF16)
            spread = jnp.dot(
                jnp.concatenate([high, low], axis=1), ones, preferred_element_type=F32
            )
            wide[pl.ds(i * 512, 512), :] = (
                shifted * lax.rsqrt(spread + epsilon) * gain_ref[...] + bias_ref[...]
            )
            return carry

        lax.fori_loop(0, I // 32, rows, 0, unroll=5)

        def turn(k, carry):
            normed[b * 16 + k] = wide[pl.ds(k, I, stride=16), :].astype(BF16)
            return carry

        lax.fori_loop(0, 16, turn, 0, unroll=8)

    def gated(tokens, weights, mask_rows):
        both = lax.dot_general(
            weights, tokens, (((1,), (1,)), ((), ())), preferred_element_type=F32
        )
        half_value, half_gate = both[:C], both[C:]
        return (half_value + half_value * jnp.tanh(half_gate)) * mask_rows

    def project_main(k, at, first):
        tokens = normed[pl.ds(k, 2), 0:128, :].reshape(256, C)
        rows = mask_main[pl.ds(k, 2), :]
        result = gated(
            tokens, proj[first : first + 2 * C, :], jnp.concatenate([rows[0:1], rows[1:2]], axis=1)
        )
        swap[pl.ds(at * C, C), :] = result[:, :128]
        swap[pl.ds(at * C + C, C), :] = result[:, 128:]

    def rest_tokens(r, low):
        return jnp.concatenate([normed[token(s, r, low), 128:, :] for s in range(4)], axis=0)

    def rest_mask(r, low):
        return by_group([mask_rest[pl.ds(token(s, r, low), 1), :] for s in range(4)])

    def project_rest(r, at, low, first):
        tokens = jnp.concatenate([rest_tokens(r, low), rest_tokens(r + 1, low)], axis=0)
        result = gated(
            tokens,
            proj[first : first + 2 * C, :],
            jnp.concatenate([rest_mask(r, low), rest_mask(r + 1, low)], axis=1),
        )
        swap[pl.ds(at * C, C), :] = result[:, :128]
        swap[pl.ds(at * C + C, C), :] = result[:, 128:]

    def ready(c):
        return

    def send_round(prepare, source, target, which):
        def one(pg, py, pcore):
            pa = py * 2 + pcore
            prepare(pg * A + pa)
            pltpu.make_async_remote_copy(
                src_ref=source(pg, pa),
                dst_ref=target,
                send_sem=send_sem.at[which],
                recv_sem=recv_sem.at[which],
                device_id=place(pg, py, pcore),
                device_id_type=MESH,
            ).start()

        prepare(mine)
        pltpu.make_async_copy(source(g, a), target, recv_sem.at[which]).start()
        each_partner(one)

    def wait_all(buffer, semaphore):
        pltpu.make_async_copy(buffer, buffer, semaphore).wait()

    def send_main(start, rows, store, target, which):
        from_row = pl.ds(by_16(start), rows)

        def prepare(c):
            store[c, from_row, :] = swap[pl.ds(c, rows, stride=C), :].astype(BF16)

        send_round(
            prepare,
            lambda pg, pa: store.at[pg * A + pa, from_row],
            target.at[a, pl.ds(by_16(g * K + start), rows)],
            which,
        )

    def project_rows(start, count, first):
        def pair(p, carry):
            project_main(start + p * 2, p * 2, first)
            return carry

        lax.fori_loop(0, count // 2, pair, 0, unroll=4)

    def left_rows(start, count):
        project_rows(start, count, 0)
        send_main(start, count, out_l, in_l, L_MAIN)

    def right_rows(start, count):
        project_rows(start, count, 2 * C)
        send_main(start, count, out_r, in_r, R_MAIN)

    def normalize_two(b):
        for n in (b, b + 1):
            fetch(n).wait()
            normalize(n)

    fetch(0).wait()
    normalize(0)
    pl.semaphore_wait(barrier, G + A - 2)
    greet_row(entry_sem)
    fetch(1).wait()
    normalize(1)
    project_rows(0, 32, 2 * C)
    pl.semaphore_wait(entry_sem, A - 1)
    send_main(0, 32, out_r, in_r, R_MAIN)
    left_rows(0, 32)
    normalize_two(2)
    right_rows(32, 32)
    fetch(4).wait()
    normalize(4)
    right_rows(64, 16)

    def low_rest(p, carry):
        project_rest(p * 2, p * 2, True, 2 * C)
        project_rest(p * 2, 16 + p * 2, True, 0)
        return carry

    lax.fori_loop(0, 8, low_rest, 0, unroll=2)

    def high_rest(p, carry):
        project_rest(p * 2, 32 + p * 2, False, 2 * C)
        project_rest(p * 2, 36 + p * 2, False, 0)
        return carry

    lax.fori_loop(0, 2, high_rest, 0, unroll=2)

    def prepare_rest(c):
        out_rest[c] = swap[pl.ds(c, BOTH, stride=C), :].astype(BF16)

    send_round(
        prepare_rest, lambda pg, pa: out_rest.at[pg * A + pa], in_rest.at[a, g], BOTH_REST
    )

    left_rows(32, 32)
    left_rows(64, 16)

    def open_gate(p, carry):
        tokens = normed[pl.ds(p * 2, 2)].reshape(2 * I, C)
        half = jnp.dot(tokens, gate_weights[...], preferred_element_type=F32)
        gates[pl.ds(p * 2, 2)] = (0.5 + 0.5 * jnp.tanh(half)).reshape(2, I, C)
        return carry

    lax.fori_loop(0, K // 2, open_gate, 0, unroll=4)

    def spread_rest(side, rest):
        def one(step, carry):
            h, sg = step >> 4, step & 15
            parts = [
                in_rest[4 * h + t, sg, 16 * side : 16 * side + 16, :].astype(F32) for t in range(4)
            ]
            tails = [in_rest[4 * h + t, sg, 32:40, :].astype(F32) for t in range(4)]
            if side:
                tails = [pltpu.roll(tail, 4, 0) for tail in tails]
            at = sg * K
            ends = []
            for n in range(4):
                rows = by_group([parts[(s + n) % 4] for s in range(4)])
                tail = by_group([tails[(s + n) % 4] for s in range(4)])
                if n:
                    rows = pltpu.roll(rows, 32 * n, 1)
                    tail = pltpu.roll(tail, 32 * n, 1)
                rest[h, pl.ds(by_16(at + n * 16), 16), :] = rows.astype(BF16)
                ends.append(tail)
            upper = lax.broadcasted_iota(jnp.int32, (8, 128), 0) < 4
            joined = jnp.concatenate(
                [
                    jnp.where(upper, ends[0], pltpu.roll(ends[1], 4, 0)),
                    jnp.where(upper, ends[2], pltpu.roll(ends[3], 4, 0)),
                ],
                axis=0,
            )
            rest[h, pl.ds(by_16(at + 64), 16), :] = joined.astype(BF16)
            return carry

        lax.fori_loop(0, 2 * G, one, 0, unroll=2)

    wait_all(in_r, recv_sem.at[R_MAIN])

    def turn_main(b, carry):
        right_t[pl.ds(pl.multiple_of(b * I, 32), 128), :] = in_r[b].T
        return carry

    lax.fori_loop(0, A, turn_main, 0)

    wait_all(in_rest, recv_sem.at[BOTH_REST])
    spread_rest(0, rest_r)

    def turn_rest(h, carry):
        turned = rest_r[h].T
        for t in range(4):
            right_t[pl.ds(pl.multiple_of((4 * h + t) * I + 128, 32), 32), :] = turned[
                32 * t : 32 * t + 32
            ]
        return carry

    lax.fori_loop(0, 2, turn_rest, 0)

    spread_rest(1, rest_l)

    def rest_product(m, carry):
        rows = right_t[pl.ds(pl.multiple_of(m * 320, 32), 320), :]
        columns = jnp.concatenate([rest_l[0], rest_l[1]], axis=1)
        product = jnp.dot(rows, columns, preferred_element_type=F32)
        for h in range(2):
            for sg in range(4):
                block = product[sg * K : (sg + 1) * K, h * 128 : (h + 1) * 128]
                mains, tails = [], []
                for n in range(4):
                    main = block[n * 16 : (n + 1) * 16]
                    tail = block[64 + 8 * (n // 2) : 72 + 8 * (n // 2)]
                    if n % 2:
                        tail = pltpu.roll(tail, 4, 0)
                    if n:
                        main = pltpu.roll(main, 128 - 32 * n, 1)
                        tail = pltpu.roll(tail, 128 - 32 * n, 1)
                    mains.append(main)
                    tails.append(tail)
                for t in range(4):
                    out_t_rest[m * 4 + sg, 4 * h + t, 0:16, :] = by_group(
                        [mains[(t - s) % 4] for s in range(4)]
                    ).astype(BF16)
                    out_t_rest[m * 4 + sg, 4 * h + t, 16:24, :] = by_group(
                        [tails[(t - s) % 4] for s in range(4)]
                    ).astype(BF16)
        return carry

    lax.fori_loop(0, 4, rest_product, 0)
    send_round(ready, lambda pg, pa: out_t_rest.at[pg, pa], in_t_rest.at[mine], T_REST)

    wait_all(in_l, recv_sem.at[L_MAIN])

    def main_product(step, carry):
        i, j = step & 3, step >> 2
        dx = (1 + 2 * i + (i >> 1)) & 3
        dy = (3 * dx + j) & 3
        tx, ty = (x + dx) & 3, (y + dy) & 3
        rows = right_t[pl.ds(pl.multiple_of(tx * 320, 32), 320), :]
        columns = jnp.concatenate([in_l[2 * ty], in_l[2 * ty + 1]], axis=1)
        product = jnp.dot(rows, columns, preferred_element_type=F32).astype(BF16)
        for h in range(2):
            out_t[pl.ds(tx * 4, 4), 2 * ty + h] = product[
                :, h * 128 : (h + 1) * 128
            ].reshape(4, K, 128)

        def send(q, carry):
            pg, pcore = tx * 4 + ((z + (q >> 1)) & 3), core ^ (q & 1)
            source = out_t.at[pg, 2 * ty + pcore, pl.ds(0, FIRST)]
            target = in_t.at[mine, pl.ds(0, FIRST)]
            own = (dx == 0) & (dy == 0) & (q == 0)

            @pl.when(own)
            def _():
                pltpu.make_async_copy(source, target, recv_sem.at[T_FIRST]).start()

            @pl.when(jnp.logical_not(own))
            def _():
                pltpu.make_async_remote_copy(
                    src_ref=source,
                    dst_ref=target,
                    send_sem=send_sem.at[T_FIRST],
                    recv_sem=recv_sem.at[T_FIRST],
                    device_id=place(pg, ty, pcore),
                    device_id_type=MESH,
                ).start()

            return carry

        lax.fori_loop(0, 8, send, 0)
        return carry

    lax.fori_loop(0, 16, main_product, 0)
    later = ((T_NEXT, pl.ds(FIRST, 16)), (T_LAST, pl.ds(FIRST + 16, 16)))
    for which, rows in later:
        send_round(ready, lambda pg, pa: out_t.at[pg, pa, rows], in_t.at[mine, rows], which)

    def settle(r, rows):
        values = swap[pl.ds(r, C, stride=rows), :]
        center = jnp.mean(values, axis=0, keepdims=True)
        shifted = values - center
        spread = jnp.mean(shifted * shifted, axis=0, keepdims=True)
        settled = (shifted * lax.rsqrt(spread + epsilon) * scaling[0] + scaling[1]).astype(BF16)
        return lax.dot_general(
            settled, ow_ref[...], (((0,), (0,)), ((), ())), preferred_element_type=F32
        )

    def widen(arrived, at, rows):
        def one(c, carry):
            swap[pl.ds(pl.multiple_of(c * rows, 8), rows), :] = arrived[
                c, pl.ds(at, rows), :
            ].astype(F32)
            return carry

        lax.fori_loop(0, C, one, 0, unroll=16)

    def finish(b, carry):
        widen(in_t, by_16(b * 16), 16)

        def one(r, carry):
            mixed = settle(r, 16)
            wide[pl.ds(pl.multiple_of(r * 128, 128), 128), :] = gates[b * 16 + r, 0:128, :] * mixed
            return carry

        lax.fori_loop(0, 16, one, 0, unroll=16)

        def turn(i, carry):
            o_ref[i, pl.ds(by_16(b * 16), 16), :] = wide[pl.ds(i, 16, stride=128), :].astype(BF16)
            return carry

        lax.fori_loop(0, 128, turn, 0, unroll=16)
        return carry

    wait_all(in_t_rest, recv_sem.at[T_REST])
    for low, count, rows, at in ((True, 16, 16, 0), (False, 4, 8, 16)):
        widen(in_t_rest, at, rows)

        def one_rest(r, carry):
            mixed = settle(r, rows)
            for s in range(4):
                j = token(s, r, low)
                late[pl.ds(pl.multiple_of(j * 32, 32), 32), :] = (
                    gates[j, 128:, :] * mixed[32 * s : 32 * s + 32]
                )
            return carry

        lax.fori_loop(0, count, one_rest, 0, unroll=4)

    def turn_late(step, carry):
        b, i = step >> 5, step & 31
        o_ref[128 + i, pl.ds(by_16(b * 16), 16), :] = late[
            pl.ds(b * 512 + i, 16, stride=32), :
        ].astype(BF16)
        return carry

    lax.fori_loop(0, 160, turn_late, 0, unroll=8)

    wait_all(in_t.at[:, pl.ds(0, FIRST)], recv_sem.at[T_FIRST])
    lax.fori_loop(0, FIRST // 16, finish, 0)

    def put(number, block):
        return pltpu.make_async_copy(
            o_ref.at[:, block], o_hbm.at[:, block], store_sem.at[number]
        )

    blocks = (pl.ds(0, FIRST),) + tuple(rows for _, rows in later)
    put(0, blocks[0]).start()
    for n, (which, rows) in enumerate(later):
        wait_all(in_t.at[:, rows], recv_sem.at[which])
        finish(FIRST // 16 + n, 0)
        put(n + 1, blocks[n + 1]).start()

    for which, buffer in (
        (R_MAIN, out_r),
        (BOTH_REST, out_rest),
        (L_MAIN, out_l),
        (T_REST, in_t_rest),
        (T_FIRST, in_t.at[:, pl.ds(0, FIRST)]),
        *((which, in_t.at[:, rows]) for which, rows in later),
    ):
        wait_all(buffer.at[pl.ds(0, 127)], send_sem.at[which])
    for n, block in enumerate(blocks):
        put(n, block).wait()


def store(from_ref, to_ref, held, sem):
    pieces = [pl.ds(n * (I // PIECES), I // PIECES) for n in range(PIECES)]
    arrive = [
        pltpu.make_async_copy(from_ref.at[piece], held.at[piece], sem.at[n])
        for n, piece in enumerate(pieces)
    ]
    leave = [
        pltpu.make_async_copy(held.at[piece], to_ref.at[piece], sem.at[n])
        for n, piece in enumerate(pieces)
    ]
    for copy in arrive:
        copy.start()
    for first, second in zip(arrive, leave):
        first.wait()
        second.start()
    for copy in leave:
        copy.wait()


def per_device(
    pair_map,
    pair_mask,
    input_gain,
    input_bias,
    input_weights,
    output_gain,
    output_bias,
    output_weight,
):
    vmem = pl.BlockSpec(memory_space=pltpu.VMEM)
    result = pl.pallas_call(
        kernel,
        out_shape=jax.ShapeDtypeStruct((I, K, C), BF16),
        in_specs=[pl.BlockSpec(memory_space=pl.ANY)] + [vmem] * 7,
        out_specs=pl.BlockSpec(memory_space=pl.ANY),
        scratch_shapes=[
            pltpu.VMEM((I, K, C), BF16),
            pltpu.VMEM((I, K, C), BF16),
            pltpu.VMEM((K * 32, C), F32),
            pltpu.VMEM((I * 16, C), F32),
            pltpu.VMEM((K, I, C), BF16),
            pltpu.VMEM((K, I, C), F32),
            pltpu.VMEM((48 * C, 128), F32),
            pltpu.VMEM((4 * C, C), BF16),
            pltpu.VMEM((C, C), BF16),
            pltpu.VMEM((K, 128), F32),
            pltpu.VMEM((K, 128), F32),
            pltpu.VMEM((2, C, 128), F32),
            pltpu.VMEM((C, K, 128), BF16),
            pltpu.VMEM((C, K, 128), BF16),
            pltpu.VMEM((G, A, K, 128), BF16),
            pltpu.VMEM((C, BOTH, 128), BF16),
            pltpu.VMEM((G, A, REST, 128), BF16),
            pltpu.VMEM((A, N, 128), BF16),
            pltpu.VMEM((A, N, 128), BF16),
            pltpu.VMEM((C, K, 128), BF16),
            pltpu.VMEM((A, G, BOTH, 128), BF16),
            pltpu.VMEM((C, REST, 128), BF16),
            pltpu.VMEM((2, N, 128), BF16),
            pltpu.VMEM((2, N, 128), BF16),
            pltpu.VMEM((N, N), BF16),
            pltpu.SemaphoreType.DMA((5,)),
            pltpu.SemaphoreType.DMA((3,)),
            pltpu.SemaphoreType.REGULAR,
            pltpu.SemaphoreType.DMA((7,)),
            pltpu.SemaphoreType.DMA((7,)),
        ],
        compiler_params=pltpu.CompilerParams(
            collective_id=0, has_side_effects=True, vmem_limit_bytes=58 * 2**20
        ),
        cost_estimate=pl.CostEstimate(
            flops=6_500_000_000, bytes_accessed=16_000_000, transcendentals=5_000_000
        ),
    )(
        pair_map,
        pair_mask,
        input_gain[None],
        input_bias[None],
        input_weights,
        output_gain[None],
        output_bias[None],
        output_weight,
    )
    anywhere = pl.BlockSpec(memory_space=pl.ANY)
    return pl.pallas_call(
        store,
        out_shape=jax.ShapeDtypeStruct((I, K, C), BF16),
        in_specs=[anywhere],
        out_specs=anywhere,
        scratch_shapes=[pltpu.VMEM((I, K, C), BF16), pltpu.SemaphoreType.DMA((PIECES,))],
        compiler_params=pltpu.CompilerParams(vmem_limit_bytes=58 * 2**20),
        cost_estimate=pl.CostEstimate(flops=0, bytes_accessed=6_600_000, transcendentals=0),
    )(result)


def solution(mesh):
    return jax.shard_map(
        per_device,
        mesh=mesh,
        in_specs=(
            P(("pr", "pc"), "grp", None),
            P(("pr", "pc"), "grp"),
            P(),
            P(),
            P(),
            P(),
            P(),
            P(),
        ),
        out_specs=P(("pr", "pc"), "grp", None),
        check_vma=False,
    )
```

```python
import jax
import jax.numpy as jnp
from jax import lax
from jax.experimental import pallas as pl
from jax.experimental.pallas import tpu as pltpu
from jax.sharding import PartitionSpec as P

MESH = pl.DeviceIdType.MESH
F32 = jnp.float32
BF16 = jnp.bfloat16
epsilon = 1e-05

I = 160
K = 80
C = 128
G = 16
A = 8
N = 1280
REST = 24
BOTH = 40
FIRST = 48
R_MAIN, BOTH_REST, L_MAIN, T_REST, T_FIRST, T_NEXT, T_LAST = range(7)


def kernel(
    x_hbm,
    mask_ref,
    gain_ref,
    bias_ref,
    weights_ref,
    ogain_ref,
    obias_ref,
    ow_ref,
    o_ref,
    x_ref,
    late,
    wide,
    normed,
    gates,
    swap,
    proj,
    gate_weights,
    mask_main,
    mask_rest,
    scaling,
    out_l,
    out_r,
    out_t,
    out_rest,
    out_t_rest,
    in_l,
    in_r,
    in_t,
    in_rest,
    in_t_rest,
    rest_l,
    rest_r,
    right_t,
    fetch_sem,
    entry_sem,
    send_sem,
    recv_sem,
):
    g = lax.axis_index("grp")
    y = lax.axis_index("pr")
    core = lax.axis_index("pc")
    x, z = g >> 2, g & 3
    a = y * 2 + core
    quarter = a & 3
    mine = g * A + a

    def partner(step):
        v = (step * 47) & 127
        w = v & 3
        px = (x + (w ^ (w >> 1))) & 3
        pcore = core ^ ((v >> 2) & 1)
        py = (y + (v >> 3)) & 3
        pz = (z + (v >> 5)) & 3
        return px * 4 + pz, py, pcore

    def place(pg, py, pcore):
        return {"grp": pg, "pr": py, "pc": pcore}

    barrier = pltpu.get_barrier_semaphore()

    def each_partner(visit):
        def several(n, carry):
            for u in range(7):
                visit(*partner(n * 7 + u + 1))
            return carry

        lax.fori_loop(0, 18, several, 0)
        visit(*partner(127))

    def fetch(b):
        block = pl.ds(b * 16, 16)
        return pltpu.make_async_copy(x_hbm.at[:, block], x_ref.at[:, block], fetch_sem.at[b])

    for b in range(5):
        fetch(b).start()

    def greet_row(semaphore):
        for step in range(1, A):
            pl.semaphore_signal(
                semaphore,
                inc=1,
                device_id=place(g, (y + (step >> 1)) & 3, core ^ (step & 1)),
                device_id_type=MESH,
            )

    def greet_column(step, carry):
        pl.semaphore_signal(
            barrier, inc=1, device_id=place((g + step) & 15, y, core), device_id_type=MESH
        )
        return carry

    lax.fori_loop(1, G, greet_column, 0, unroll=5)
    greet_row(barrier)

    def by_group(parts):
        group = lax.broadcasted_iota(jnp.int32, parts[0].shape, 1) // 32
        return jnp.where(
            group == 0,
            parts[0],
            jnp.where(group == 1, parts[1], jnp.where(group == 2, parts[2], parts[3])),
        )

    def token(s, r, low):
        n = (quarter - s + 4) & 3
        return n * 16 + r if low else 64 + n * 4 + r

    def by_16(value):
        return pl.multiple_of(value, 16)

    for part in range(4):
        columns = weights_ref[:, part * C : (part + 1) * C].astype(F32)
        proj[part * C : (part + 1) * C, :] = (0.5 * columns.T).astype(BF16)
    gate_weights[...] = (0.5 * weights_ref[:, 4 * C :].astype(F32)).astype(BF16)
    scaling[0] = jnp.broadcast_to(ogain_ref[...], (C, 128)).T
    scaling[1] = jnp.broadcast_to(obias_ref[...], (C, 128)).T
    mask = mask_ref[...].astype(F32).T
    mask_main[...] = mask[:, :128]
    mask_rest[...] = jnp.concatenate([mask[:, 128:]] * 4, axis=1)
    ones = jnp.full((256, 128), 1 / 128, BF16)

    def normalize(b):
        def rows(i, carry):
            block = x_ref[pl.ds(i * 32, 32), pl.ds(by_16(b * 16), 16), :].reshape(512, C)
            center = jnp.dot(block, ones[:128], preferred_element_type=F32)
            shifted = block.astype(F32) - center
            squares = shifted * shifted
            high = squares.astype(BF16)
            low = (squares - high.astype(F32)).astype(BF16)
            spread = jnp.dot(
                jnp.concatenate([high, low], axis=1), ones, preferred_element_type=F32
            )
            wide[pl.ds(i * 512, 512), :] = (
                shifted * lax.rsqrt(spread + epsilon) * gain_ref[...] + bias_ref[...]
            )
            return carry

        lax.fori_loop(0, I // 32, rows, 0, unroll=5)

        def turn(k, carry):
            normed[b * 16 + k] = wide[pl.ds(k, I, stride=16), :].astype(BF16)
            return carry

        lax.fori_loop(0, 16, turn, 0, unroll=8)

    def gated(tokens, weights, mask_rows):
        both = lax.dot_general(
            weights, tokens, (((1,), (1,)), ((), ())), preferred_element_type=F32
        )
        half_value, half_gate = both[:C], both[C:]
        return (half_value + half_value * jnp.tanh(half_gate)) * mask_rows

    def project_main(k, at, first):
        tokens = normed[pl.ds(k, 2), 0:128, :].reshape(256, C)
        rows = mask_main[pl.ds(k, 2), :]
        result = gated(
            tokens, proj[first : first + 2 * C, :], jnp.concatenate([rows[0:1], rows[1:2]], axis=1)
        )
        swap[pl.ds(at * C, C), :] = result[:, :128]
        swap[pl.ds(at * C + C, C), :] = result[:, 128:]

    def rest_tokens(r, low):
        return jnp.concatenate([normed[token(s, r, low), 128:, :] for s in range(4)], axis=0)

    def rest_mask(r, low):
        return by_group([mask_rest[pl.ds(token(s, r, low), 1), :] for s in range(4)])

    def project_rest(r, at, low, first):
        tokens = jnp.concatenate([rest_tokens(r, low), rest_tokens(r + 1, low)], axis=0)
        result = gated(
            tokens,
            proj[first : first + 2 * C, :],
            jnp.concatenate([rest_mask(r, low), rest_mask(r + 1, low)], axis=1),
        )
        swap[pl.ds(at * C, C), :] = result[:, :128]
        swap[pl.ds(at * C + C, C), :] = result[:, 128:]

    def ready(c):
        return

    def send_round(prepare, source, target, which):
        def one(pg, py, pcore):
            pa = py * 2 + pcore
            prepare(pg * A + pa)
            pltpu.make_async_remote_copy(
                src_ref=source(pg, pa),
                dst_ref=target,
                send_sem=send_sem.at[which],
                recv_sem=recv_sem.at[which],
                device_id=place(pg, py, pcore),
                device_id_type=MESH,
            ).start()

        prepare(mine)
        pltpu.make_async_copy(source(g, a), target, recv_sem.at[which]).start()
        each_partner(one)

    def wait_all(buffer, semaphore):
        pltpu.make_async_copy(buffer, buffer, semaphore).wait()

    def send_main(start, rows, store, target, which):
        from_row = pl.ds(by_16(start), rows)

        def prepare(c):
            store[c, from_row, :] = swap[pl.ds(c, rows, stride=C), :].astype(BF16)

        send_round(
            prepare,
            lambda pg, pa: store.at[pg * A + pa, from_row],
            target.at[a, pl.ds(by_16(g * K + start), rows)],
            which,
        )

    def project_rows(start, count, first):
        def pair(p, carry):
            project_main(start + p * 2, p * 2, first)
            return carry

        lax.fori_loop(0, count // 2, pair, 0, unroll=4)

    def left_rows(start, count):
        project_rows(start, count, 0)
        send_main(start, count, out_l, in_l, L_MAIN)

    def right_rows(start, count):
        project_rows(start, count, 2 * C)
        send_main(start, count, out_r, in_r, R_MAIN)

    def normalize_two(b):
        for n in (b, b + 1):
            fetch(n).wait()
            normalize(n)

    fetch(0).wait()
    normalize(0)
    pl.semaphore_wait(barrier, G + A - 2)
    greet_row(entry_sem)
    project_rows(0, 16, 2 * C)
    pl.semaphore_wait(entry_sem, A - 1)
    send_main(0, 16, out_r, in_r, R_MAIN)
    left_rows(0, 16)
    for b in range(2):
        normalize_two(2 * b + 1)
        right_rows(32 * b + 16, 32)

    def low_rest(p, carry):
        project_rest(p * 2, p * 2, True, 2 * C)
        project_rest(p * 2, 16 + p * 2, True, 0)
        return carry

    lax.fori_loop(0, 8, low_rest, 0, unroll=2)

    def high_rest(p, carry):
        project_rest(p * 2, 32 + p * 2, False, 2 * C)
        project_rest(p * 2, 36 + p * 2, False, 0)
        return carry

    lax.fori_loop(0, 2, high_rest, 0, unroll=2)

    def prepare_rest(c):
        out_rest[c] = swap[pl.ds(c, BOTH, stride=C), :].astype(BF16)

    send_round(
        prepare_rest, lambda pg, pa: out_rest.at[pg * A + pa], in_rest.at[a, g], BOTH_REST
    )

    left_rows(16, 32)
    left_rows(48, 32)

    def open_gate(p, carry):
        tokens = normed[pl.ds(p * 2, 2)].reshape(2 * I, C)
        half = jnp.dot(tokens, gate_weights[...], preferred_element_type=F32)
        gates[pl.ds(p * 2, 2)] = (0.5 + 0.5 * jnp.tanh(half)).reshape(2, I, C)
        return carry

    lax.fori_loop(0, K // 2, open_gate, 0, unroll=4)

    def spread_rest(side, rest):
        def one(step, carry):
            h, sg = step >> 4, step & 15
            parts = [
                in_rest[4 * h + t, sg, 16 * side : 16 * side + 16, :].astype(F32) for t in range(4)
            ]
            tails = [in_rest[4 * h + t, sg, 32:40, :].astype(F32) for t in range(4)]
            if side:
                tails = [pltpu.roll(tail, 4, 0) for tail in tails]
            at = sg * K
            ends = []
            for n in range(4):
                rows = by_group([parts[(s + n) % 4] for s in range(4)])
                tail = by_group([tails[(s + n) % 4] for s in range(4)])
                if n:
                    rows = pltpu.roll(rows, 32 * n, 1)
                    tail = pltpu.roll(tail, 32 * n, 1)
                rest[h, pl.ds(by_16(at + n * 16), 16), :] = rows.astype(BF16)
                ends.append(tail)
            upper = lax.broadcasted_iota(jnp.int32, (8, 128), 0) < 4
            joined = jnp.concatenate(
                [
                    jnp.where(upper, ends[0], pltpu.roll(ends[1], 4, 0)),
                    jnp.where(upper, ends[2], pltpu.roll(ends[3], 4, 0)),
                ],
                axis=0,
            )
            rest[h, pl.ds(by_16(at + 64), 16), :] = joined.astype(BF16)
            return carry

        lax.fori_loop(0, 2 * G, one, 0, unroll=2)

    wait_all(in_r, recv_sem.at[R_MAIN])

    def turn_main(b, carry):
        right_t[pl.ds(pl.multiple_of(b * I, 32), 128), :] = in_r[b].T
        return carry

    lax.fori_loop(0, A, turn_main, 0)

    wait_all(in_rest, recv_sem.at[BOTH_REST])
    spread_rest(0, rest_r)

    def turn_rest(h, carry):
        turned = rest_r[h].T
        for t in range(4):
            right_t[pl.ds(pl.multiple_of((4 * h + t) * I + 128, 32), 32), :] = turned[
                32 * t : 32 * t + 32
            ]
        return carry

    lax.fori_loop(0, 2, turn_rest, 0)

    spread_rest(1, rest_l)

    def rest_product(m, carry):
        rows = right_t[pl.ds(pl.multiple_of(m * 320, 32), 320), :]
        columns = jnp.concatenate([rest_l[0], rest_l[1]], axis=1)
        product = jnp.dot(rows, columns, preferred_element_type=F32)
        for h in range(2):
            for sg in range(4):
                block = product[sg * K : (sg + 1) * K, h * 128 : (h + 1) * 128]
                mains, tails = [], []
                for n in range(4):
                    main = block[n * 16 : (n + 1) * 16]
                    tail = block[64 + 8 * (n // 2) : 72 + 8 * (n // 2)]
                    if n % 2:
                        tail = pltpu.roll(tail, 4, 0)
                    if n:
                        main = pltpu.roll(main, 128 - 32 * n, 1)
                        tail = pltpu.roll(tail, 128 - 32 * n, 1)
                    mains.append(main)
                    tails.append(tail)
                for t in range(4):
                    out_t_rest[m * 4 + sg, 4 * h + t, 0:16, :] = by_group(
                        [mains[(t - s) % 4] for s in range(4)]
                    ).astype(BF16)
                    out_t_rest[m * 4 + sg, 4 * h + t, 16:24, :] = by_group(
                        [tails[(t - s) % 4] for s in range(4)]
                    ).astype(BF16)
        return carry

    lax.fori_loop(0, 4, rest_product, 0)
    send_round(ready, lambda pg, pa: out_t_rest.at[pg, pa], in_t_rest.at[mine], T_REST)

    wait_all(in_l, recv_sem.at[L_MAIN])

    def main_product(step, carry):
        i, j = step & 3, step >> 2
        dx = (1 + 2 * i + (i >> 1)) & 3
        dy = (3 * dx + j) & 3
        tx, ty = (x + dx) & 3, (y + dy) & 3
        rows = right_t[pl.ds(pl.multiple_of(tx * 320, 32), 320), :]
        columns = jnp.concatenate([in_l[2 * ty], in_l[2 * ty + 1]], axis=1)
        product = jnp.dot(rows, columns, preferred_element_type=F32).astype(BF16)
        for h in range(2):
            out_t[pl.ds(tx * 4, 4), 2 * ty + h] = product[
                :, h * 128 : (h + 1) * 128
            ].reshape(4, K, 128)

        def send(q, carry):
            pg, pcore = tx * 4 + ((z + (q >> 1)) & 3), core ^ (q & 1)
            source = out_t.at[pg, 2 * ty + pcore, pl.ds(0, FIRST)]
            target = in_t.at[mine, pl.ds(0, FIRST)]
            own = (dx == 0) & (dy == 0) & (q == 0)

            @pl.when(own)
            def _():
                pltpu.make_async_copy(source, target, recv_sem.at[T_FIRST]).start()

            @pl.when(jnp.logical_not(own))
            def _():
                pltpu.make_async_remote_copy(
                    src_ref=source,
                    dst_ref=target,
                    send_sem=send_sem.at[T_FIRST],
                    recv_sem=recv_sem.at[T_FIRST],
                    device_id=place(pg, ty, pcore),
                    device_id_type=MESH,
                ).start()

            return carry

        lax.fori_loop(0, 8, send, 0)
        return carry

    lax.fori_loop(0, 16, main_product, 0)
    later = ((T_NEXT, pl.ds(FIRST, 16)), (T_LAST, pl.ds(FIRST + 16, 16)))
    for which, rows in later:
        send_round(ready, lambda pg, pa: out_t.at[pg, pa, rows], in_t.at[mine, rows], which)

    def settle(r, rows):
        values = swap[pl.ds(r, C, stride=rows), :]
        center = jnp.mean(values, axis=0, keepdims=True)
        shifted = values - center
        spread = jnp.mean(shifted * shifted, axis=0, keepdims=True)
        settled = (shifted * lax.rsqrt(spread + epsilon) * scaling[0] + scaling[1]).astype(BF16)
        return lax.dot_general(
            settled, ow_ref[...], (((0,), (0,)), ((), ())), preferred_element_type=F32
        )

    def widen(arrived, at, rows):
        def one(c, carry):
            swap[pl.ds(pl.multiple_of(c * rows, 8), rows), :] = arrived[
                c, pl.ds(at, rows), :
            ].astype(F32)
            return carry

        lax.fori_loop(0, C, one, 0, unroll=16)

    def finish(b, carry):
        widen(in_t, by_16(b * 16), 16)

        def one(r, carry):
            mixed = settle(r, 16)
            wide[pl.ds(pl.multiple_of(r * 128, 128), 128), :] = gates[b * 16 + r, 0:128, :] * mixed
            return carry

        lax.fori_loop(0, 16, one, 0, unroll=16)

        def turn(i, carry):
            o_ref[i, pl.ds(by_16(b * 16), 16), :] = wide[pl.ds(i, 16, stride=128), :].astype(BF16)
            return carry

        lax.fori_loop(0, 128, turn, 0, unroll=16)
        return carry

    wait_all(in_t_rest, recv_sem.at[T_REST])
    for low, count, rows, at in ((True, 16, 16, 0), (False, 4, 8, 16)):
        widen(in_t_rest, at, rows)

        def one_rest(r, carry):
            mixed = settle(r, rows)
            for s in range(4):
                j = token(s, r, low)
                late[pl.ds(pl.multiple_of(j * 32, 32), 32), :] = (
                    gates[j, 128:, :] * mixed[32 * s : 32 * s + 32]
                )
            return carry

        lax.fori_loop(0, count, one_rest, 0, unroll=4)

    def turn_late(step, carry):
        b, i = step >> 5, step & 31
        o_ref[128 + i, pl.ds(by_16(b * 16), 16), :] = late[
            pl.ds(b * 512 + i, 16, stride=32), :
        ].astype(BF16)
        return carry

    lax.fori_loop(0, 160, turn_late, 0, unroll=8)

    wait_all(in_t.at[:, pl.ds(0, FIRST)], recv_sem.at[T_FIRST])
    lax.fori_loop(0, FIRST // 16, finish, 0)
    for n, (which, rows) in enumerate(later):
        wait_all(in_t.at[:, rows], recv_sem.at[which])
        finish(FIRST // 16 + n, 0)

    for which, buffer in (
        (R_MAIN, out_r),
        (BOTH_REST, out_rest),
        (L_MAIN, out_l),
        (T_REST, in_t_rest),
        (T_FIRST, in_t.at[:, pl.ds(0, FIRST)]),
        *((which, in_t.at[:, rows]) for which, rows in later),
    ):
        wait_all(buffer.at[pl.ds(0, 127)], send_sem.at[which])


def per_device(
    pair_map,
    pair_mask,
    input_gain,
    input_bias,
    input_weights,
    output_gain,
    output_bias,
    output_weight,
):
    vmem = pl.BlockSpec(memory_space=pltpu.VMEM)
    result = pl.pallas_call(
        kernel,
        out_shape=pltpu.VMEM((I, K, C), BF16),
        in_specs=[pl.BlockSpec(memory_space=pl.ANY)] + [vmem] * 7,
        out_specs=vmem,
        scratch_shapes=[
            pltpu.VMEM((I, K, C), BF16),
            pltpu.VMEM((K * 32, C), F32),
            pltpu.VMEM((I * 16, C), F32),
            pltpu.VMEM((K, I, C), BF16),
            pltpu.VMEM((K, I, C), F32),
            pltpu.VMEM((48 * C, 128), F32),
            pltpu.VMEM((4 * C, C), BF16),
            pltpu.VMEM((C, C), BF16),
            pltpu.VMEM((K, 128), F32),
            pltpu.VMEM((K, 128), F32),
            pltpu.VMEM((2, C, 128), F32),
            pltpu.VMEM((C, K, 128), BF16),
            pltpu.VMEM((C, K, 128), BF16),
            pltpu.VMEM((G, A, K, 128), BF16),
            pltpu.VMEM((C, BOTH, 128), BF16),
            pltpu.VMEM((G, A, REST, 128), BF16),
            pltpu.VMEM((A, N, 128), BF16),
            pltpu.VMEM((A, N, 128), BF16),
            pltpu.VMEM((C, K, 128), BF16),
            pltpu.VMEM((A, G, BOTH, 128), BF16),
            pltpu.VMEM((C, REST, 128), BF16),
            pltpu.VMEM((2, N, 128), BF16),
            pltpu.VMEM((2, N, 128), BF16),
            pltpu.VMEM((N, N), BF16),
            pltpu.SemaphoreType.DMA((5,)),
            pltpu.SemaphoreType.REGULAR,
            pltpu.SemaphoreType.DMA((7,)),
            pltpu.SemaphoreType.DMA((7,)),
        ],
        compiler_params=pltpu.CompilerParams(
            collective_id=0, has_side_effects=True, vmem_limit_bytes=58 * 2**20
        ),
        cost_estimate=pl.CostEstimate(
            flops=6_500_000_000, bytes_accessed=16_000_000, transcendentals=5_000_000
        ),
    )(
        pair_map,
        pair_mask,
        input_gain[None],
        input_bias[None],
        input_weights,
        output_gain[None],
        output_bias[None],
        output_weight,
    )
    return result


def solution(mesh):
    return jax.shard_map(
        per_device,
        mesh=mesh,
        in_specs=(
            P(("pr", "pc"), "grp", None),
            P(("pr", "pc"), "grp"),
            P(),
            P(),
            P(),
            P(),
            P(),
            P(),
        ),
        out_specs=P(("pr", "pc"), "grp", None),
        check_vma=False,
    )
```

```python
import jax
import jax.numpy as jnp
from jax import lax
from jax.experimental import pallas as pl
from jax.experimental.pallas import tpu as pltpu
from jax.sharding import PartitionSpec as P

MESH = pl.DeviceIdType.MESH
F32 = jnp.float32
BF16 = jnp.bfloat16
epsilon = 1e-05

I = 160
K = 80
C = 128
G = 16
A = 8
N = 1280
REST = 24
BOTH = 40
FIRST = 48
R_MAIN, BOTH_REST, L_MAIN, T_REST, T_FIRST, T_NEXT, T_LAST = range(7)


def kernel(
    x_hbm,
    mask_hbm,
    gain_hbm,
    bias_hbm,
    weights_hbm,
    ogain_hbm,
    obias_hbm,
    ow_hbm,
    o_ref,
    x_ref,
    mask_ref,
    gain_ref,
    bias_ref,
    weights_ref,
    ogain_ref,
    obias_ref,
    ow_ref,
    late,
    wide,
    normed,
    gates,
    swap,
    proj,
    gate_weights,
    mask_main,
    mask_rest,
    scaling,
    out_l,
    out_r,
    out_t,
    out_rest,
    out_t_rest,
    in_l,
    in_r,
    in_t,
    in_rest,
    in_t_rest,
    rest_l,
    rest_r,
    right_t,
    fetch_sem,
    small_sem,
    entry_sem,
    send_sem,
    recv_sem,
):
    g = lax.axis_index("grp")
    y = lax.axis_index("pr")
    core = lax.axis_index("pc")
    x, z = g >> 2, g & 3
    a = y * 2 + core
    quarter = a & 3
    mine = g * A + a

    def partner(step):
        v = (step * 47) & 127
        w = v & 3
        px = (x + (w ^ (w >> 1))) & 3
        pcore = core ^ ((v >> 2) & 1)
        py = (y + (v >> 3)) & 3
        pz = (z + (v >> 5)) & 3
        return px * 4 + pz, py, pcore

    def place(pg, py, pcore):
        return {"grp": pg, "pr": py, "pc": pcore}

    barrier = pltpu.get_barrier_semaphore()

    def each_partner(visit):
        def several(n, carry):
            for u in range(7):
                visit(*partner(n * 7 + u + 1))
            return carry

        lax.fori_loop(0, 18, several, 0)
        visit(*partner(127))

    smalls = [
        pltpu.make_async_copy(source, target, small_sem.at[n])
        for n, (source, target) in enumerate(
            (
                (weights_hbm, weights_ref),
                (mask_hbm, mask_ref),
                (gain_hbm, gain_ref),
                (bias_hbm, bias_ref),
                (ogain_hbm, ogain_ref),
                (obias_hbm, obias_ref),
                (ow_hbm, ow_ref),
            )
        )
    ]

    def fetch(b):
        block = pl.ds(b * 16, 16)
        return pltpu.make_async_copy(x_hbm.at[:, block], x_ref.at[:, block], fetch_sem.at[b])

    for b in range(5):
        fetch(b).start()
    for copy in smalls:
        copy.start()

    def greet_row(semaphore):
        for step in range(1, A):
            pl.semaphore_signal(
                semaphore,
                inc=1,
                device_id=place(g, (y + (step >> 1)) & 3, core ^ (step & 1)),
                device_id_type=MESH,
            )

    def greet_column(step, carry):
        pl.semaphore_signal(
            barrier, inc=1, device_id=place((g + step) & 15, y, core), device_id_type=MESH
        )
        return carry

    lax.fori_loop(1, G, greet_column, 0, unroll=5)
    greet_row(barrier)

    def by_group(parts):
        group = lax.broadcasted_iota(jnp.int32, parts[0].shape, 1) // 32
        return jnp.where(
            group == 0,
            parts[0],
            jnp.where(group == 1, parts[1], jnp.where(group == 2, parts[2], parts[3])),
        )

    def token(s, r, low):
        n = (quarter - s + 4) & 3
        return n * 16 + r if low else 64 + n * 4 + r

    def by_16(value):
        return pl.multiple_of(value, 16)

    for copy in smalls:
        copy.wait()

    for part in range(4):
        columns = weights_ref[:, part * C : (part + 1) * C].astype(F32)
        proj[part * C : (part + 1) * C, :] = (0.5 * columns.T).astype(BF16)
    gate_weights[...] = (0.5 * weights_ref[:, 4 * C :].astype(F32)).astype(BF16)
    scaling[0] = jnp.broadcast_to(ogain_ref[...], (C, 128)).T
    scaling[1] = jnp.broadcast_to(obias_ref[...], (C, 128)).T
    mask = mask_ref[...].astype(F32).T
    mask_main[...] = mask[:, :128]
    mask_rest[...] = jnp.concatenate([mask[:, 128:]] * 4, axis=1)
    ones = jnp.full((256, 128), 1 / 128, BF16)

    def normalize(b):
        def rows(i, carry):
            block = x_ref[pl.ds(i * 32, 32), pl.ds(by_16(b * 16), 16), :].reshape(512, C)
            center = jnp.dot(block, ones[:128], preferred_element_type=F32)
            shifted = block.astype(F32) - center
            squares = shifted * shifted
            high = squares.astype(BF16)
            low = (squares - high.astype(F32)).astype(BF16)
            spread = jnp.dot(
                jnp.concatenate([high, low], axis=1), ones, preferred_element_type=F32
            )
            wide[pl.ds(i * 512, 512), :] = (
                shifted * lax.rsqrt(spread + epsilon) * gain_ref[...] + bias_ref[...]
            )
            return carry

        lax.fori_loop(0, I // 32, rows, 0, unroll=5)

        def turn(k, carry):
            normed[b * 16 + k] = wide[pl.ds(k, I, stride=16), :].astype(BF16)
            return carry

        lax.fori_loop(0, 16, turn, 0, unroll=8)

    def gated(tokens, weights, mask_rows):
        both = lax.dot_general(
            weights, tokens, (((1,), (1,)), ((), ())), preferred_element_type=F32
        )
        half_value, half_gate = both[:C], both[C:]
        return (half_value + half_value * jnp.tanh(half_gate)) * mask_rows

    def project_main(k, at, first):
        tokens = normed[pl.ds(k, 2), 0:128, :].reshape(256, C)
        rows = mask_main[pl.ds(k, 2), :]
        result = gated(
            tokens, proj[first : first + 2 * C, :], jnp.concatenate([rows[0:1], rows[1:2]], axis=1)
        )
        swap[pl.ds(at * C, C), :] = result[:, :128]
        swap[pl.ds(at * C + C, C), :] = result[:, 128:]

    def rest_tokens(r, low):
        return jnp.concatenate([normed[token(s, r, low), 128:, :] for s in range(4)], axis=0)

    def rest_mask(r, low):
        return by_group([mask_rest[pl.ds(token(s, r, low), 1), :] for s in range(4)])

    def project_rest(r, at, low, first):
        tokens = jnp.concatenate([rest_tokens(r, low), rest_tokens(r + 1, low)], axis=0)
        result = gated(
            tokens,
            proj[first : first + 2 * C, :],
            jnp.concatenate([rest_mask(r, low), rest_mask(r + 1, low)], axis=1),
        )
        swap[pl.ds(at * C, C), :] = result[:, :128]
        swap[pl.ds(at * C + C, C), :] = result[:, 128:]

    def ready(c):
        return

    def send_round(prepare, source, target, which):
        def one(pg, py, pcore):
            pa = py * 2 + pcore
            prepare(pg * A + pa)
            pltpu.make_async_remote_copy(
                src_ref=source(pg, pa),
                dst_ref=target,
                send_sem=send_sem.at[which],
                recv_sem=recv_sem.at[which],
                device_id=place(pg, py, pcore),
                device_id_type=MESH,
            ).start()

        prepare(mine)
        pltpu.make_async_copy(source(g, a), target, recv_sem.at[which]).start()
        each_partner(one)

    def wait_all(buffer, semaphore):
        pltpu.make_async_copy(buffer, buffer, semaphore).wait()

    def send_main(start, rows, store, target, which):
        from_row = pl.ds(by_16(start), rows)

        def prepare(c):
            store[c, from_row, :] = swap[pl.ds(c, rows, stride=C), :].astype(BF16)

        send_round(
            prepare,
            lambda pg, pa: store.at[pg * A + pa, from_row],
            target.at[a, pl.ds(by_16(g * K + start), rows)],
            which,
        )

    def project_rows(start, count, first):
        def pair(p, carry):
            project_main(start + p * 2, p * 2, first)
            return carry

        lax.fori_loop(0, count // 2, pair, 0, unroll=4)

    def left_rows(start, count):
        project_rows(start, count, 0)
        send_main(start, count, out_l, in_l, L_MAIN)

    def right_rows(start, count):
        project_rows(start, count, 2 * C)
        send_main(start, count, out_r, in_r, R_MAIN)

    def normalize_two(b):
        for n in (b, b + 1):
            fetch(n).wait()
            normalize(n)

    fetch(0).wait()
    normalize(0)
    pl.semaphore_wait(barrier, G + A - 2)
    greet_row(entry_sem)
    project_rows(0, 16, 2 * C)
    pl.semaphore_wait(entry_sem, A - 1)
    send_main(0, 16, out_r, in_r, R_MAIN)
    left_rows(0, 16)
    for b in range(2):
        normalize_two(2 * b + 1)
        right_rows(32 * b + 16, 32)

    def low_rest(p, carry):
        project_rest(p * 2, p * 2, True, 2 * C)
        project_rest(p * 2, 16 + p * 2, True, 0)
        return carry

    lax.fori_loop(0, 8, low_rest, 0, unroll=2)

    def high_rest(p, carry):
        project_rest(p * 2, 32 + p * 2, False, 2 * C)
        project_rest(p * 2, 36 + p * 2, False, 0)
        return carry

    lax.fori_loop(0, 2, high_rest, 0, unroll=2)

    def prepare_rest(c):
        out_rest[c] = swap[pl.ds(c, BOTH, stride=C), :].astype(BF16)

    send_round(
        prepare_rest, lambda pg, pa: out_rest.at[pg * A + pa], in_rest.at[a, g], BOTH_REST
    )

    left_rows(16, 32)
    left_rows(48, 32)

    def open_gate(p, carry):
        tokens = normed[pl.ds(p * 2, 2)].reshape(2 * I, C)
        half = jnp.dot(tokens, gate_weights[...], preferred_element_type=F32)
        gates[pl.ds(p * 2, 2)] = (0.5 + 0.5 * jnp.tanh(half)).reshape(2, I, C)
        return carry

    lax.fori_loop(0, K // 2, open_gate, 0, unroll=4)

    def spread_rest(side, rest):
        def one(step, carry):
            h, sg = step >> 4, step & 15
            parts = [
                in_rest[4 * h + t, sg, 16 * side : 16 * side + 16, :].astype(F32) for t in range(4)
            ]
            tails = [in_rest[4 * h + t, sg, 32:40, :].astype(F32) for t in range(4)]
            if side:
                tails = [pltpu.roll(tail, 4, 0) for tail in tails]
            at = sg * K
            ends = []
            for n in range(4):
                rows = by_group([parts[(s + n) % 4] for s in range(4)])
                tail = by_group([tails[(s + n) % 4] for s in range(4)])
                if n:
                    rows = pltpu.roll(rows, 32 * n, 1)
                    tail = pltpu.roll(tail, 32 * n, 1)
                rest[h, pl.ds(by_16(at + n * 16), 16), :] = rows.astype(BF16)
                ends.append(tail)
            upper = lax.broadcasted_iota(jnp.int32, (8, 128), 0) < 4
            joined = jnp.concatenate(
                [
                    jnp.where(upper, ends[0], pltpu.roll(ends[1], 4, 0)),
                    jnp.where(upper, ends[2], pltpu.roll(ends[3], 4, 0)),
                ],
                axis=0,
            )
            rest[h, pl.ds(by_16(at + 64), 16), :] = joined.astype(BF16)
            return carry

        lax.fori_loop(0, 2 * G, one, 0, unroll=2)

    wait_all(in_r, recv_sem.at[R_MAIN])

    def turn_main(b, carry):
        right_t[pl.ds(pl.multiple_of(b * I, 32), 128), :] = in_r[b].T
        return carry

    lax.fori_loop(0, A, turn_main, 0)

    wait_all(in_rest, recv_sem.at[BOTH_REST])
    spread_rest(0, rest_r)

    def turn_rest(h, carry):
        turned = rest_r[h].T
        for t in range(4):
            right_t[pl.ds(pl.multiple_of((4 * h + t) * I + 128, 32), 32), :] = turned[
                32 * t : 32 * t + 32
            ]
        return carry

    lax.fori_loop(0, 2, turn_rest, 0)

    spread_rest(1, rest_l)

    def rest_product(m, carry):
        rows = right_t[pl.ds(pl.multiple_of(m * 320, 32), 320), :]
        columns = jnp.concatenate([rest_l[0], rest_l[1]], axis=1)
        product = jnp.dot(rows, columns, preferred_element_type=F32)
        for h in range(2):
            for sg in range(4):
                block = product[sg * K : (sg + 1) * K, h * 128 : (h + 1) * 128]
                mains, tails = [], []
                for n in range(4):
                    main = block[n * 16 : (n + 1) * 16]
                    tail = block[64 + 8 * (n // 2) : 72 + 8 * (n // 2)]
                    if n % 2:
                        tail = pltpu.roll(tail, 4, 0)
                    if n:
                        main = pltpu.roll(main, 128 - 32 * n, 1)
                        tail = pltpu.roll(tail, 128 - 32 * n, 1)
                    mains.append(main)
                    tails.append(tail)
                for t in range(4):
                    out_t_rest[m * 4 + sg, 4 * h + t, 0:16, :] = by_group(
                        [mains[(t - s) % 4] for s in range(4)]
                    ).astype(BF16)
                    out_t_rest[m * 4 + sg, 4 * h + t, 16:24, :] = by_group(
                        [tails[(t - s) % 4] for s in range(4)]
                    ).astype(BF16)
        return carry

    lax.fori_loop(0, 4, rest_product, 0)
    send_round(ready, lambda pg, pa: out_t_rest.at[pg, pa], in_t_rest.at[mine], T_REST)

    wait_all(in_l, recv_sem.at[L_MAIN])

    def main_product(step, carry):
        i, j = step & 3, step >> 2
        dx = (1 + 2 * i + (i >> 1)) & 3
        dy = (3 * dx + j) & 3
        tx, ty = (x + dx) & 3, (y + dy) & 3
        rows = right_t[pl.ds(pl.multiple_of(tx * 320, 32), 320), :]
        columns = jnp.concatenate([in_l[2 * ty], in_l[2 * ty + 1]], axis=1)
        product = jnp.dot(rows, columns, preferred_element_type=F32).astype(BF16)
        for h in range(2):
            out_t[pl.ds(tx * 4, 4), 2 * ty + h] = product[
                :, h * 128 : (h + 1) * 128
            ].reshape(4, K, 128)

        def send(q, carry):
            pg, pcore = tx * 4 + ((z + (q >> 1)) & 3), core ^ (q & 1)
            source = out_t.at[pg, 2 * ty + pcore, pl.ds(0, FIRST)]
            target = in_t.at[mine, pl.ds(0, FIRST)]
            own = (dx == 0) & (dy == 0) & (q == 0)

            @pl.when(own)
            def _():
                pltpu.make_async_copy(source, target, recv_sem.at[T_FIRST]).start()

            @pl.when(jnp.logical_not(own))
            def _():
                pltpu.make_async_remote_copy(
                    src_ref=source,
                    dst_ref=target,
                    send_sem=send_sem.at[T_FIRST],
                    recv_sem=recv_sem.at[T_FIRST],
                    device_id=place(pg, ty, pcore),
                    device_id_type=MESH,
                ).start()

            return carry

        lax.fori_loop(0, 8, send, 0)
        return carry

    lax.fori_loop(0, 16, main_product, 0)
    later = ((T_NEXT, pl.ds(FIRST, 16)), (T_LAST, pl.ds(FIRST + 16, 16)))
    for which, rows in later:
        send_round(ready, lambda pg, pa: out_t.at[pg, pa, rows], in_t.at[mine, rows], which)

    def settle(r, rows):
        values = swap[pl.ds(r, C, stride=rows), :]
        center = jnp.mean(values, axis=0, keepdims=True)
        shifted = values - center
        spread = jnp.mean(shifted * shifted, axis=0, keepdims=True)
        settled = (shifted * lax.rsqrt(spread + epsilon) * scaling[0] + scaling[1]).astype(BF16)
        return lax.dot_general(
            settled, ow_ref[...], (((0,), (0,)), ((), ())), preferred_element_type=F32
        )

    def widen(arrived, at, rows):
        def one(c, carry):
            swap[pl.ds(pl.multiple_of(c * rows, 8), rows), :] = arrived[
                c, pl.ds(at, rows), :
            ].astype(F32)
            return carry

        lax.fori_loop(0, C, one, 0, unroll=16)

    def finish(b, carry):
        widen(in_t, by_16(b * 16), 16)

        def one(r, carry):
            mixed = settle(r, 16)
            wide[pl.ds(pl.multiple_of(r * 128, 128), 128), :] = gates[b * 16 + r, 0:128, :] * mixed
            return carry

        lax.fori_loop(0, 16, one, 0, unroll=16)

        def turn(i, carry):
            o_ref[i, pl.ds(by_16(b * 16), 16), :] = wide[pl.ds(i, 16, stride=128), :].astype(BF16)
            return carry

        lax.fori_loop(0, 128, turn, 0, unroll=16)
        return carry

    wait_all(in_t_rest, recv_sem.at[T_REST])
    for low, count, rows, at in ((True, 16, 16, 0), (False, 4, 8, 16)):
        widen(in_t_rest, at, rows)

        def one_rest(r, carry):
            mixed = settle(r, rows)
            for s in range(4):
                j = token(s, r, low)
                late[pl.ds(pl.multiple_of(j * 32, 32), 32), :] = (
                    gates[j, 128:, :] * mixed[32 * s : 32 * s + 32]
                )
            return carry

        lax.fori_loop(0, count, one_rest, 0, unroll=4)

    def turn_late(step, carry):
        b, i = step >> 5, step & 31
        o_ref[128 + i, pl.ds(by_16(b * 16), 16), :] = late[
            pl.ds(b * 512 + i, 16, stride=32), :
        ].astype(BF16)
        return carry

    lax.fori_loop(0, 160, turn_late, 0, unroll=8)

    wait_all(in_t.at[:, pl.ds(0, FIRST)], recv_sem.at[T_FIRST])
    lax.fori_loop(0, FIRST // 16, finish, 0)
    for n, (which, rows) in enumerate(later):
        wait_all(in_t.at[:, rows], recv_sem.at[which])
        finish(FIRST // 16 + n, 0)

    for which, buffer in (
        (R_MAIN, out_r),
        (BOTH_REST, out_rest),
        (L_MAIN, out_l),
        (T_REST, in_t_rest),
        (T_FIRST, in_t.at[:, pl.ds(0, FIRST)]),
        *((which, in_t.at[:, rows]) for which, rows in later),
    ):
        wait_all(buffer.at[pl.ds(0, 127)], send_sem.at[which])


def per_device(
    pair_map,
    pair_mask,
    input_gain,
    input_bias,
    input_weights,
    output_gain,
    output_bias,
    output_weight,
):
    vmem = pl.BlockSpec(memory_space=pltpu.VMEM)
    result = pl.pallas_call(
        kernel,
        out_shape=pltpu.VMEM((I, K, C), BF16),
        in_specs=[pl.BlockSpec(memory_space=pl.ANY)] * 8,
        out_specs=vmem,
        scratch_shapes=[
            pltpu.VMEM((I, K, C), BF16),
            pltpu.VMEM((I, K), jnp.int32),
            pltpu.VMEM((1, C), F32),
            pltpu.VMEM((1, C), F32),
            pltpu.VMEM((C, 5 * C), BF16),
            pltpu.VMEM((1, C), F32),
            pltpu.VMEM((1, C), F32),
            pltpu.VMEM((C, C), BF16),
            pltpu.VMEM((K * 32, C), F32),
            pltpu.VMEM((I * 16, C), F32),
            pltpu.VMEM((K, I, C), BF16),
            pltpu.VMEM((K, I, C), F32),
            pltpu.VMEM((48 * C, 128), F32),
            pltpu.VMEM((4 * C, C), BF16),
            pltpu.VMEM((C, C), BF16),
            pltpu.VMEM((K, 128), F32),
            pltpu.VMEM((K, 128), F32),
            pltpu.VMEM((2, C, 128), F32),
            pltpu.VMEM((C, K, 128), BF16),
            pltpu.VMEM((C, K, 128), BF16),
            pltpu.VMEM((G, A, K, 128), BF16),
            pltpu.VMEM((C, BOTH, 128), BF16),
            pltpu.VMEM((G, A, REST, 128), BF16),
            pltpu.VMEM((A, N, 128), BF16),
            pltpu.VMEM((A, N, 128), BF16),
            pltpu.VMEM((C, K, 128), BF16),
            pltpu.VMEM((A, G, BOTH, 128), BF16),
            pltpu.VMEM((C, REST, 128), BF16),
            pltpu.VMEM((2, N, 128), BF16),
            pltpu.VMEM((2, N, 128), BF16),
            pltpu.VMEM((N, N), BF16),
            pltpu.SemaphoreType.DMA((5,)),
            pltpu.SemaphoreType.DMA((7,)),
            pltpu.SemaphoreType.REGULAR,
            pltpu.SemaphoreType.DMA((7,)),
            pltpu.SemaphoreType.DMA((7,)),
        ],
        compiler_params=pltpu.CompilerParams(
            collective_id=0, has_side_effects=True, vmem_limit_bytes=58 * 2**20
        ),
        cost_estimate=pl.CostEstimate(
            flops=6_500_000_000, bytes_accessed=16_000_000, transcendentals=5_000_000
        ),
    )(
        pair_map,
        pair_mask,
        input_gain[None],
        input_bias[None],
        input_weights,
        output_gain[None],
        output_bias[None],
        output_weight,
    )
    return result


def solution(mesh):
    return jax.shard_map(
        per_device,
        mesh=mesh,
        in_specs=(
            P(("pr", "pc"), "grp", None),
            P(("pr", "pc"), "grp"),
            P(),
            P(),
            P(),
            P(),
            P(),
            P(),
        ),
        out_specs=P(("pr", "pc"), "grp", None),
        check_vma=False,
    )
```
